32 devices in a mesh: dp: 8 (over z, y), tensor: 4 (over x, core).
Axes of the slice: x: 2, y: 2, z: 4, core: 2. Of those that a mesh axis runs over, the one named last changes fastest.
Arguments:
- layer_input: bfloat16 [8192, 4096], P(('dp', 'tensor')), may hold values from -6 to 6
- kv_weight: bfloat16 [2, 4096, 1024], P(None, None, 'tensor'), may hold values from -0.09375 to 0.09375
- kv_cotangent: bfloat16 [2, 8192, 1024], P(None, 'dp', 'tensor'), may hold values from -6 to 6
- error_before: bfloat16 [8, 2, 4096, 1024], P('dp', None, None, 'tensor'), may hold values from -6 to 6
- right_factor: float32 [2, 32, 4096], replicated, may hold values from -6 to 6
Outputs:
- error_after: float32 [8, 2, 4096, 1024], P('dp', None, None, 'tensor')
- right_next: float32 [2, 32, 4096], replicated
- input_grad: bfloat16 [8192, 4096], P(('dp', 'tensor'))
The draws below stay inside these ranges and needn't reach their ends.
All inputs are finite; a program needn't handle non-finite values.
Results may differ from the reference program's by a relative error of at most 0.012.
Values may be sent and summed in bfloat16 or wider, within the bound.
No kernel may reach another device: no remote copies, remote signals or barrier semaphores. Data moves between devices by JAX's collectives and lax.ppermute only.
A program may use at most 128 MiB of HBM per device.

```python
from functools import partial
import jax
import jax.numpy as jnp
from jax import lax

D = 4096
RANK = 32
TOKENS = 1024
C = 1024
ROWS = 8192
N_DP = 8
N_TENSOR = 4


def shard_levels(own_key, dims, cuts, least, top_value):
    loudness, own = 1.0, jax.random.fold_in(own_key, 6)
    for position, blocks in cuts:
        heights = jnp.exp(jax.random.uniform(jax.random.fold_in(own, position), (blocks,), jnp.float32, least / len(cuts), top_value / len(cuts)))
        loudness = loudness * jnp.repeat(heights, dims[position] // blocks).reshape([-1 if axis == position else 1 for axis in range(len(dims))])
    return loudness


def scatter_about(rng, shape, deviation, reach, shards=(), held_as=jnp.bfloat16):
    entries = jax.random.normal(rng, shape, jnp.float32) * deviation
    if len(shards) > 0:
        entries = shard_levels(rng, shape, shards, -0.22, 0.18) * entries
    return jnp.clip(entries, min=-reach, max=reach).astype(held_as)


def setup_inputs(seed: int = 0) -> dict:
    seeds = jax.random.split(jax.random.key(seed), 6)
    return {
        "layer_input": scatter_about(seeds[0], (ROWS, D), 1.0, 6.0, ((0, 32),)),
        "kv_weight": scatter_about(seeds[1], (2, D, C), D ** -0.5, 0.09375, ((2, 4),)),
        "kv_cotangent": scatter_about(seeds[2], (2, ROWS, C), 1.0, 6.0, ((1, 8), (2, 4))),
        "error_before": scatter_about(seeds[3], (N_DP, 2, D, C), 1.0, 6.0, ((0, 8), (3, 4))),
        "right_factor": scatter_about(seeds[4], (2, RANK, D), 1.0, 6.0, (), jnp.float32),
    }


def replica_moment(input_rows, grad_rows, error_rows):
    product = jnp.einsum('td,mtc->mdc', input_rows.astype(jnp.float32), grad_rows.astype(jnp.float32))
    return product * TOKENS ** (-0.5) + error_rows.astype(jnp.float32)

def replica_input_grad(grad_rows, kv_weight):
    grad_groups = grad_rows.astype(jnp.float32).reshape(2, TOKENS, N_TENSOR, C // N_TENSOR)
    weight_groups = kv_weight.astype(jnp.float32).reshape(2, D, N_TENSOR, C // N_TENSOR)
    partials = jnp.einsum('mtkc,mdkc->ktd', grad_groups, weight_groups)
    partials = partials.astype(jnp.bfloat16).astype(jnp.float32)
    return lax.optimization_barrier(jnp.sum(partials, axis=0)).astype(jnp.bfloat16)

def reference(layer_input, kv_weight, kv_cotangent, error_before, right_factor):
    highest = lax.Precision.HIGHEST
    input_rows = layer_input.reshape(N_DP, TOKENS, D)
    grad_rows = jnp.transpose(kv_cotangent.reshape(2, N_DP, TOKENS, C), (1, 0, 2, 3))
    moments = lax.map(lambda items: replica_moment(items[0], items[1], items[2]), (input_rows, grad_rows, error_before))
    left_sum = jnp.einsum('nmdc,mrd->mrc', moments, right_factor, precision=highest)
    gram_matrix = jnp.einsum('mrc,msc->mrs', left_sum, left_sum, precision=highest)
    factor = jnp.linalg.cholesky(gram_matrix)
    ortho_basis = jax.vmap(partial(jax.scipy.linalg.solve_triangular, lower=True))(factor, left_sum)
    right_next = jnp.einsum('nmdc,mrc->mrd', moments, ortho_basis, precision=highest) / N_DP
    approximation = jnp.einsum('mrd,mrc->mdc', right_next, ortho_basis, precision=highest)
    error_after = moments - approximation[None]
    input_grad = lax.map(lambda rows: replica_input_grad(rows, kv_weight), grad_rows)
    return (error_after, right_next, input_grad.reshape(ROWS, D))
```

```python
from functools import partial

import jax
import jax.numpy as jnp
from jax import lax
from jax.experimental import pallas as pl
from jax.experimental.pallas import tpu as pltpu
from jax.sharding import PartitionSpec as P

TOKENS = 1024
SCALE = TOKENS ** (-0.5)
F32, BF16 = jnp.float32, jnp.bfloat16
VMEM_LIMIT = 48 * 1024 * 1024
NN = (((1,), (0,)), ((), ()))
NT = (((1,), (1,)), ((), ()))
TN = (((0,), (0,)), ((), ()))
HIGHEST = lax.Precision.HIGHEST


def mm(a, b, dims, precision=None):
    return lax.dot_general(a, b, dims, precision=precision, preferred_element_type=F32)


def split(value, terms):
    parts, rest = [], value
    for _ in range(terms):
        part = rest.astype(BF16)
        parts.append(part)
        rest = rest - part.astype(F32)
    return jnp.concatenate(parts, axis=0)


def split_mm(a, b, dims, terms):
    rows = a.shape[0]
    product = mm(split(a, terms), b, dims)
    total = product[:rows]
    for k in range(1, terms):
        total = total + product[k * rows : (k + 1) * rows]
    return total


def params(*semantics):
    return pltpu.CompilerParams(
        vmem_limit_bytes=VMEM_LIMIT,
        dimension_semantics=semantics if semantics else None,
    )


def cost(flops, nbytes):
    return pl.CostEstimate(flops=int(flops), bytes_accessed=int(nbytes), transcendentals=0)


def project_kernel(x_ref, r_ref, y_ref):
    modes, rank, chunk = r_ref.shape
    term = split_mm(r_ref[...].reshape(modes * rank, chunk), x_ref[...], NT, 3)

    @pl.when(pl.program_id(0) == 0)
    def _():
        y_ref[...] = term

    @pl.when(pl.program_id(0) > 0)
    def _():
        y_ref[...] += term


def project(x, r, chunk=1024):
    rows, depth = x.shape
    modes, rank, _ = r.shape
    return pl.pallas_call(
        project_kernel,
        grid=(depth // chunk,),
        in_specs=[
            pl.BlockSpec((rows, chunk), lambda i: (0, i)),
            pl.BlockSpec((modes, rank, chunk), lambda i: (0, 0, i)),
        ],
        out_specs=pl.BlockSpec((modes * rank, rows), lambda i: (0, 0)),
        out_shape=jax.ShapeDtypeStruct((modes * rank, rows), F32),
        compiler_params=params("arbitrary"),
        cost_estimate=cost(6 * rows * depth * modes * rank, x.nbytes + r.nbytes),
        name="project",
    )(x, r)


def feedback_kernel(r_ref, e_ref, out_ref):
    term = split_mm(r_ref[0], e_ref[0], NN, 3)

    @pl.when(pl.program_id(1) == 0)
    def _():
        out_ref[...] = term

    @pl.when(pl.program_id(1) > 0)
    def _():
        out_ref[...] += term


def feedback(r, e, chunk=2048):
    modes, rank, depth = r.shape
    cols = e.shape[-1]
    return pl.pallas_call(
        feedback_kernel,
        grid=(modes, depth // chunk),
        in_specs=[
            pl.BlockSpec((1, rank, chunk), lambda m, i: (m, 0, i)),
            pl.BlockSpec((1, chunk, cols), lambda m, i: (m, i, 0)),
        ],
        out_specs=pl.BlockSpec((rank, cols), lambda m, i: (m, 0)),
        out_shape=jax.ShapeDtypeStruct((modes * rank, cols), F32),
        compiler_params=params("arbitrary", "arbitrary"),
        cost_estimate=cost(6 * modes * rank * depth * cols, r.nbytes + e.nbytes),
        name="feedback",
    )(r, e)


def rows_of(t_ref, j, rows):
    return pl.ds(pl.multiple_of((t_ref[0] ^ j) * rows, rows), rows)


def left_kernel(t_ref, y0, y1, y2, y3, g_ref, e_ref, out_ref):
    modes = g_ref.shape[0]
    rank, rows = y0.shape[0] // modes, y0.shape[1]
    for m in range(modes):
        at = slice(m * rank, (m + 1) * rank)
        total = 0.0
        for j, y in enumerate((y0, y1, y2, y3)):
            total = total + split_mm(y[at, :], g_ref[m, rows_of(t_ref, j, rows), :], NN, 3)
        out_ref[at, :] = total * SCALE + e_ref[at, :]


SMEM = pl.BlockSpec(memory_space=pltpu.SMEM)
VMEM = pl.BlockSpec(memory_space=pltpu.VMEM)


def left_local(t, ys, g, e):
    return pl.pallas_call(
        left_kernel,
        in_specs=[SMEM] + [VMEM] * 6,
        out_specs=VMEM,
        out_shape=jax.ShapeDtypeStruct(e.shape, F32),
        compiler_params=params(),
        cost_estimate=cost(6 * e.size * 1024, g.nbytes),
        name="left",
    )(t, *ys, g, e)


def spread_kernel(t_ref, left_ref, g_ref, keep_ref, send_ref):
    modes = g_ref.shape[0]
    rank = left_ref.shape[0] // modes
    rows = g_ref.shape[1] // 4
    for j, (ref, at) in enumerate(((keep_ref, 0), (send_ref, 0), (keep_ref, 1), (send_ref, 1))):
        for m in range(modes):
            top = (at * modes + m) * rank
            ref[top : top + rank, :] = split_mm(
                left_ref[m * rank : (m + 1) * rank, :], g_ref[m, rows_of(t_ref, j, rows), :], NT, 3
            )
    zero = jnp.zeros((rank, left_ref.shape[1]), F32)
    a, b = left_ref[0:rank, :], left_ref[rank : 2 * rank, :]
    gram = mm(a, jnp.concatenate([a, zero, zero, zero], axis=0), NT, HIGHEST)
    gram = gram + mm(b, jnp.concatenate([zero, zero, b, zero], axis=0), NT, HIGHEST)
    top = 2 * modes * rank
    for ref in (keep_ref, send_ref):
        ref[top:, 0:128] = gram
        ref[top:, 128:] = jnp.zeros((rank, rows - 128), F32)


def spread(t, left, g):
    shape = jax.ShapeDtypeStruct((2 * left.shape[0] + left.shape[0] // 2, g.shape[1] // 4), F32)
    return pl.pallas_call(
        spread_kernel,
        in_specs=[SMEM, VMEM, VMEM],
        out_specs=[VMEM, VMEM],
        out_shape=[shape, shape],
        compiler_params=params(),
        cost_estimate=cost(6 * left.size * 1024, g.nbytes),
        name="spread",
    )(t, left, g)


def solve_kernel(sum_ref, got_ref, left_ref, z_ref, b_ref):
    modes = 2
    rank = left_ref.shape[0] // modes
    n = modes * rank
    gram = sum_ref[n:, 0:128] + got_ref[n:, 0:128]
    row = lax.broadcasted_iota(jnp.int32, (rank, 128), 0)
    lane = lax.broadcasted_iota(jnp.int32, (rank, 128), 1)
    ones = jnp.where((lane == row + rank) | (lane == row + 3 * rank), 1.0, 0.0)
    a = jnp.where((lane // rank) % 2 == 0, gram, ones)
    low = lane < 2 * rank
    scale = jnp.zeros((rank, 128), F32)
    for k in range(rank):
        pivot_row = a[k : k + 1, :]
        column = jnp.where(low, a[:, k : k + 1], a[:, 2 * rank + k : 2 * rank + k + 1])
        pivot = column[k : k + 1, :]
        inverse = 1.0 / pivot
        scale = jnp.where(row == k, lax.rsqrt(pivot), scale)
        a = jnp.where(row > k, a - column * (inverse * pivot_row), a)
    a = a * scale
    zero = jnp.zeros((rank, left_ref.shape[1]), F32)
    z = (sum_ref[0:n, :] + got_ref[0:n, :]) * SCALE
    for m in range(modes):
        part = jnp.where(lane // rank == 2 * m + 1, a, 0.0)
        at = slice(m * rank, (m + 1) * rank)
        for value, ref in ((z[at], z_ref), (left_ref[at, :], b_ref)):
            stacked = [zero] * 4
            stacked[2 * m + 1] = value
            ref[at, :] = mm(part, jnp.concatenate(stacked, axis=0), NN, HIGHEST)


def solve(summed, got, left):
    shape = jax.ShapeDtypeStruct(left.shape, F32)
    return pl.pallas_call(
        solve_kernel,
        in_specs=[VMEM, VMEM, VMEM],
        out_specs=[VMEM, VMEM],
        out_shape=[shape, shape],
        compiler_params=params(),
        cost_estimate=cost(10**7, 10**7),
        name="solve",
    )(summed, got, left)


def right_kernel(h_ref, z_ref, b_ref, x_ref, e_ref, out_ref):
    modes = e_ref.shape[0]
    rank = z_ref.shape[0] // modes
    out_ref[...] = split_mm(z_ref[...], x_ref[...], NN, 2)
    for m in range(modes):
        at = slice(m * rank, (m + 1) * rank)
        out_ref[at, :] += split_mm(b_ref[at, :], e_ref[m], NT, 2)


def right_half(half, z, b, x, e, chunk=512):
    rows, depth = x.shape
    modes, _, cols = e.shape
    steps = depth // 2 // chunk
    return pl.pallas_call(
        right_kernel,
        grid_spec=pltpu.PrefetchScalarGridSpec(
            num_scalar_prefetch=1,
            grid=(steps,),
            in_specs=[
                pl.BlockSpec(z.shape, lambda i, h: (0, 0)),
                pl.BlockSpec(b.shape, lambda i, h: (0, 0)),
                pl.BlockSpec((rows, chunk), lambda i, h: (0, h[0] * steps + i)),
                pl.BlockSpec((modes, chunk, cols), lambda i, h: (0, h[0] * steps + i, 0)),
            ],
            out_specs=pl.BlockSpec((z.shape[0], chunk), lambda i, h: (0, i)),
        ),
        out_shape=jax.ShapeDtypeStruct((z.shape[0], depth // 2), F32),
        compiler_params=params("arbitrary"),
        cost_estimate=cost(4 * depth * rows * 128, x.nbytes // 2 + e.nbytes // 2),
        name="right",
    )(half, z, b, x, e)


def moment_kernel(t_ref, x0, x1, x2, x3, g_ref, e_ref, out_ref):
    modes = g_ref.shape[0]
    rows = x0.shape[0]
    for m in range(modes):
        total = 0.0
        for j, x in enumerate((x0, x1, x2, x3)):
            total = total + mm(x[...], g_ref[m, rows_of(t_ref, j, rows), :], TN)
        out_ref[m] = total * SCALE + e_ref[m].astype(F32)


def moment(t, xs, g, e, chunk=512):
    rows, depth = xs[0].shape
    modes, tokens, cols = g.shape
    return pl.pallas_call(
        moment_kernel,
        grid=(depth // chunk,),
        in_specs=[SMEM]
        + [pl.BlockSpec((rows, chunk), lambda i: (0, i))] * 4
        + [
            pl.BlockSpec((modes, tokens, cols), lambda i: (0, 0, 0)),
            pl.BlockSpec((modes, chunk, cols), lambda i: (0, i, 0)),
        ],
        out_specs=pl.BlockSpec((modes, chunk, cols), lambda i: (0, i, 0)),
        out_shape=jax.ShapeDtypeStruct((modes, depth, cols), F32),
        compiler_params=params("arbitrary"),
        cost_estimate=cost(2 * tokens * depth * modes * cols, 24 * 2**20),
        name="moment",
    )(t, *xs, g, e)


def error_kernel(m_ref, right_ref, b_ref, out_ref):
    modes = m_ref.shape[0]
    rank = b_ref.shape[0] // modes
    for m in range(modes):
        at = slice(m * rank, (m + 1) * rank)
        high = right_ref[at, :].astype(BF16)
        b = b_ref[at, :]
        b0 = b.astype(BF16)
        b1 = (b - b0.astype(F32)).astype(BF16)
        product = mm(jnp.concatenate([high, high], axis=0), jnp.concatenate([b0, b1], axis=0), TN)
        out_ref[m] = m_ref[m] - product


def error_after(moments, right, b, chunk=512):
    modes, depth, cols = moments.shape
    spec = pl.BlockSpec((modes, chunk, cols), lambda i: (0, i, 0))
    return pl.pallas_call(
        error_kernel,
        grid=(depth // chunk,),
        in_specs=[
            spec,
            pl.BlockSpec((right.shape[0], chunk), lambda i: (0, i)),
            pl.BlockSpec(b.shape, lambda i: (0, 0)),
        ],
        out_specs=spec,
        out_shape=jax.ShapeDtypeStruct(moments.shape, F32),
        input_output_aliases={0: 0},
        compiler_params=params("arbitrary"),
        cost_estimate=cost(2 * depth * modes * cols * 64, 2 * moments.nbytes),
        name="error_after",
    )(moments, right, b)


def grad_kernel(j, n, t_ref, g_ref, w_ref, *refs):
    more, out_ref = refs[:n], refs[n]
    rows = out_ref.shape[0]
    at = rows_of(t_ref, j, rows)
    total = mm(g_ref[0, at, :], w_ref[0], NT) + mm(g_ref[1, at, :], w_ref[1], NT)
    for ref in more:
        total = total + ref[...].astype(F32)
    out_ref[...] = total.astype(BF16)


def grad_block(t, g, w, j, more=(), chunk=1024):
    modes, depth, cols = w.shape
    rows = g.shape[1] // 4
    spec = pl.BlockSpec((rows, chunk), lambda i: (0, i))
    return pl.pallas_call(
        partial(grad_kernel, j, len(more)),
        grid=(depth // chunk,),
        in_specs=[
            SMEM,
            pl.BlockSpec(g.shape, lambda i: (0, 0, 0)),
            pl.BlockSpec((modes, chunk, cols), lambda i: (0, i, 0)),
        ]
        + [spec] * len(more),
        out_specs=spec,
        out_shape=jax.ShapeDtypeStruct((rows, depth), BF16),
        compiler_params=params("arbitrary"),
        cost_estimate=cost(2 * rows * depth * modes * cols, w.nbytes),
        name="grad_block",
    )(t, g, w, *more)


def compress(moments, right_prev):
    highest = lax.Precision.HIGHEST
    replicas = lax.axis_size("dp")
    projected = jnp.einsum("mdc,mrd->mrc", moments, right_prev, precision=highest)
    left_sum = lax.psum(projected, "dp")
    gram_matrix = lax.psum(
        jnp.einsum("mrc,msc->mrs", left_sum, left_sum, precision=highest), "tensor"
    )
    factor = jnp.linalg.cholesky(gram_matrix)
    ortho_basis = jax.vmap(partial(jax.scipy.linalg.solve_triangular, lower=True))(factor, left_sum)
    right_local = jnp.einsum("mdc,mrc->mrd", moments, ortho_basis, precision=highest)
    right_total = lax.psum(right_local, "tensor")
    right_total = lax.psum(right_total, "dp")
    right_mean = right_total / replicas
    approximation = jnp.einsum("mrd,mrc->mdc", right_mean, ortho_basis, precision=highest)
    return (moments - approximation, right_mean)


def any_mesh(layer_input, kv_weight, kv_cotangent, error_before, right_factor):
    portion = kv_cotangent
    weight_grad = jnp.einsum(
        "td,mtc->mdc",
        lax.all_gather(layer_input, "tensor", axis=0, tiled=True),
        portion,
        preferred_element_type=jnp.float32,
    )
    moments = weight_grad * TOKENS ** (-0.5) + error_before[0].astype(jnp.float32)
    portion = kv_cotangent
    input_sum = lax.psum_scatter(
        jnp.einsum("mtc,mdc->td", portion, kv_weight, preferred_element_type=jnp.float32).astype(
            jnp.bfloat16
        ),
        "tensor",
        scatter_dimension=0,
        tiled=True,
    )
    leading = compress(moments[0:1], right_factor[0:1])
    second = compress(moments[1:2], right_factor[1:2])
    errors = jnp.concatenate([leading[0], second[0]], axis=0)
    right_next = jnp.concatenate([leading[1], second[1]], axis=0)
    return (errors[None], right_next, input_sum)


def per_device(layer_input, kv_weight, kv_cotangent, error_before, right_factor):
    tensor, replicas = lax.axis_size("tensor"), lax.axis_size("dp")
    t = lax.axis_index("tensor").astype(jnp.int32)
    t_arr = t.reshape(1)
    core, xpos = t % 2, t // 2
    errors = error_before[0]
    n = 2 * right_factor.shape[1]

    def over(value, axis, bit):
        size = tensor if axis == "tensor" else replicas
        return lax.ppermute(value, axis, [(i, i ^ bit) for i in range(size)])

    y0 = project(layer_input, right_factor)
    x1 = over(layer_input, "tensor", 1)
    x2 = over(layer_input, "tensor", 2)
    y1 = over(y0, "tensor", 1)
    pair = over(jnp.concatenate([y0, y1], axis=0), "tensor", 2)
    e = feedback(right_factor, errors)
    left = left_local(t_arr, (y0, y1, pair[:n], pair[n:]), kv_cotangent, e)
    bit = 1
    while bit < replicas:
        left = left + over(left, "dp", bit)
        bit *= 2

    keep, send = spread(t_arr, left, kv_cotangent)
    summed = keep + over(send, "tensor", 1)
    mine, away = summed[:n], summed[n:]
    got = over(away, "tensor", 2)
    whole = jnp.concatenate([mine, away[n:]], axis=0)
    z, b = solve(whole, got, left)

    half_send = right_half((1 - core).reshape(1), z, b, layer_input, errors)
    half_got = over(half_send, "tensor", 1)
    half = right_half(core.reshape(1), z, b, layer_input, errors) + half_got
    quarter = half.shape[1] // 2
    give = lax.dynamic_slice_in_dim(half, (1 - xpos) * quarter, quarter, 1).astype(BF16)
    own = lax.dynamic_slice_in_dim(half, xpos * quarter, quarter, 1)
    own = own + over(give, "tensor", 2).astype(F32)
    bit = 1
    while bit < replicas:
        rounded = lax.optimization_barrier(own.astype(BF16))
        own = rounded.astype(F32) + over(rounded, "dp", bit).astype(F32)
        bit *= 2
    rounded = lax.optimization_barrier((own * (1.0 / replicas)).astype(BF16))
    other = over(rounded, "tensor", 2)
    both = jnp.where(
        xpos == 0,
        jnp.concatenate([rounded, other], axis=1),
        jnp.concatenate([other, rounded], axis=1),
    )
    sibling = over(both, "tensor", 1)
    right = jnp.where(
        core == 0,
        jnp.concatenate([both, sibling], axis=1),
        jnp.concatenate([sibling, both], axis=1),
    ).astype(F32)

    p3 = grad_block(t_arr, kv_cotangent, kv_weight, 3)
    s2 = grad_block(t_arr, kv_cotangent, kv_weight, 2, (over(p3, "tensor", 1),))
    far = over(s2, "tensor", 2)
    p1 = grad_block(t_arr, kv_cotangent, kv_weight, 1)
    near = over(p1, "tensor", 1)
    input_grad = grad_block(t_arr, kv_cotangent, kv_weight, 0, (near, far))

    x3 = over(x2, "tensor", 1)
    moments = moment(t_arr, (layer_input, x1, x2, x3), kv_cotangent, errors)
    after = error_after(moments, right, b)
    return (after[None], right.reshape(right_factor.shape), input_grad)


def solution(mesh):
    sizes = mesh.shape
    fits = sizes["tensor"] == 4 and sizes["dp"] & (sizes["dp"] - 1) == 0
    return jax.shard_map(
        per_device if fits else any_mesh,
        mesh=mesh,
        in_specs=(
            P(("dp", "tensor"), None),
            P(None, None, "tensor"),
            P(None, "dp", "tensor"),
            P("dp", None, None, "tensor"),
            P(),
        ),
        out_specs=(P("dp", None, None, "tensor"), P(), P(("dp", "tensor"), None)),
        check_vma=False,
    )
```

```python
from functools import partial

import jax
import jax.numpy as jnp
from jax import lax
from jax.experimental import pallas as pl
from jax.experimental.pallas import tpu as pltpu
from jax.sharding import PartitionSpec as P

TOKENS = 1024
SCALE = TOKENS ** (-0.5)
F32, BF16 = jnp.float32, jnp.bfloat16
WEIGHT = 4096
SECOND_PIECES = (1, 3)
VMEM_LIMIT = 20 * 1024 * 1024
NN = (((1,), (0,)), ((), ()))
NT = (((1,), (1,)), ((), ()))
TN = (((0,), (0,)), ((), ()))
HIGHEST = lax.Precision.HIGHEST


def mm(a, b, dims, precision=None):
    return lax.dot_general(a, b, dims, precision=precision, preferred_element_type=F32)


def split(value, terms):
    parts, rest = [], value
    for _ in range(terms):
        part = rest.astype(BF16)
        parts.append(part)
        rest = rest - part.astype(F32)
    return jnp.concatenate(parts, axis=0)


def split_mm(a, b, dims, terms):
    rows = a.shape[0]
    product = mm(split(a, terms), b, dims)
    total = product[:rows]
    for k in range(1, terms):
        total = total + product[k * rows : (k + 1) * rows]
    return total


def params(*semantics):
    return pltpu.CompilerParams(
        vmem_limit_bytes=VMEM_LIMIT,
        dimension_semantics=semantics if semantics else None,
    )


SMEM = pl.BlockSpec(memory_space=pltpu.SMEM)
VMEM = pl.BlockSpec(memory_space=pltpu.VMEM)


def hbm(value):
    return pltpu.with_memory_space_constraint(value, pltpu.HBM)


def cost(flops, nbytes):
    return pl.CostEstimate(flops=int(flops) // WEIGHT, bytes_accessed=int(nbytes) // WEIGHT, transcendentals=0)


def project_kernel(x_ref, r_ref, y_ref):
    modes, rank, chunk = r_ref.shape
    term = split_mm(r_ref[...].reshape(modes * rank, chunk), x_ref[...], NT, 3)

    @pl.when(pl.program_id(0) == 0)
    def _():
        y_ref[...] = term

    @pl.when(pl.program_id(0) > 0)
    def _():
        y_ref[...] += term


def project(x, r, chunk=2048):
    rows, depth = x.shape
    modes, rank, _ = r.shape
    return pl.pallas_call(
        project_kernel,
        grid=(depth // chunk,),
        in_specs=[
            pl.BlockSpec((rows, chunk), lambda i: (0, i)),
            pl.BlockSpec((modes, rank, chunk), lambda i: (0, 0, i)),
        ],
        out_specs=pl.BlockSpec((modes * rank, rows), lambda i: (0, 0)),
        out_shape=jax.ShapeDtypeStruct((modes * rank, rows), F32),
        compiler_params=params("arbitrary"),
        cost_estimate=cost(6 * rows * depth * modes * rank, x.nbytes + r.nbytes),
        name="project",
    )(hbm(x), hbm(r))


def feedback_kernel(r_ref, e_ref, out_ref):
    term = split_mm(r_ref[0], e_ref[0], NN, 3)

    @pl.when(pl.program_id(1) == 0)
    def _():
        out_ref[...] = term

    @pl.when(pl.program_id(1) > 0)
    def _():
        out_ref[...] += term


def feedback(r, e, chunk=2048):
    modes, rank, depth = r.shape
    cols = e.shape[-1]
    return pl.pallas_call(
        feedback_kernel,
        grid=(modes, depth // chunk),
        in_specs=[
            pl.BlockSpec((1, rank, chunk), lambda m, i: (m, 0, i)),
            pl.BlockSpec((1, chunk, cols), lambda m, i: (m, i, 0)),
        ],
        out_specs=pl.BlockSpec((rank, cols), lambda m, i: (m, 0)),
        out_shape=jax.ShapeDtypeStruct((modes * rank, cols), F32),
        compiler_params=params("arbitrary", "arbitrary"),
        cost_estimate=cost(6 * modes * rank * depth * cols, r.nbytes + e.nbytes),
        name="feedback",
    )(hbm(r), hbm(e))


def rows_of(t_ref, j, rows):
    return pl.ds(pl.multiple_of((t_ref[0] ^ j) * rows, rows), rows)


def by_core(t_ref, on_core0, on_core1):
    return jnp.where(t_ref[0] % 2 == 0, on_core0, on_core1)


def left_kernel(t_ref, own, near, far0, far1, g_ref, e_ref, out_ref):
    modes = g_ref.shape[0]
    rank, rows = own.shape[0] // modes, own.shape[1]
    n = modes * rank
    far = by_core(t_ref, far0[...], far1[...])
    same = by_core(t_ref, far[n:], far[:n])
    other = by_core(t_ref, far[:n], far[n:])
    for m in range(modes):
        at = slice(m * rank, (m + 1) * rank)
        total = 0.0
        for j, y in enumerate((own[...], near[...], same, other)):
            total = total + split_mm(y[at], g_ref[m, rows_of(t_ref, j, rows), :], NN, 3)
        out_ref[at, :] = total * SCALE + e_ref[at, :]


def left_local(t, ys, g, e):
    return pl.pallas_call(
        left_kernel,
        in_specs=[SMEM] + [VMEM] * 6,
        out_specs=VMEM,
        out_shape=jax.ShapeDtypeStruct(e.shape, F32),
        compiler_params=params(),
        cost_estimate=cost(6 * e.size * g.shape[1], g.nbytes),
        name="left",
    )(t, *ys, g, e)


def spread_kernel(t_ref, left_ref, g_ref, own_ref, near_ref, far_ref):
    modes = g_ref.shape[0]
    rank = left_ref.shape[0] // modes
    rows = own_ref.shape[1]
    n = modes * rank
    low = 2 + t_ref[0] % 2
    for j, (ref, top) in ((0, (own_ref, 0)), (1, (near_ref, 0)), (low, (far_ref, 0)), (low ^ 1, (far_ref, n))):
        for m in range(modes):
            ref[top + m * rank : top + (m + 1) * rank, :] = split_mm(
                left_ref[m * rank : (m + 1) * rank, :], g_ref[m, rows_of(t_ref, j, rows), :], NT, 3
            )
    zero = jnp.zeros((rank, left_ref.shape[1]), F32)
    a, b = left_ref[0:rank, :], left_ref[rank : 2 * rank, :]
    gram = mm(a, jnp.concatenate([a, zero, zero, zero], axis=0), NT, HIGHEST)
    gram = gram + mm(b, jnp.concatenate([zero, zero, b, zero], axis=0), NT, HIGHEST)
    far_ref[2 * n :, 0:128] = gram
    far_ref[2 * n :, 128:] = jnp.zeros((rank, rows - 128), F32)


def spread(t, left, g):
    rows = g.shape[1] // 4
    n = left.shape[0]
    small = jax.ShapeDtypeStruct((n, rows), F32)
    return pl.pallas_call(
        spread_kernel,
        in_specs=[SMEM, VMEM, VMEM],
        out_specs=[VMEM, VMEM, VMEM],
        out_shape=[small, small, jax.ShapeDtypeStruct((2 * n + n // 2, rows), F32)],
        compiler_params=params(),
        cost_estimate=cost(6 * left.size * g.shape[1], g.nbytes),
        name="spread",
    )(t, left, g)


def solve_kernel(t_ref, own_ref, near_ref, chip_ref, got0, got1, left_ref, z_ref, b_ref):
    modes = 2
    rank = left_ref.shape[0] // modes
    n = modes * rank
    got = by_core(t_ref, got0[...], got1[...])
    gram = chip_ref[2 * n :, 0:128] + got[2 * n :, 0:128]
    row = lax.broadcasted_iota(jnp.int32, (rank, 128), 0)
    lane = lax.broadcasted_iota(jnp.int32, (rank, 128), 1)
    ones = jnp.where((lane == row + rank) | (lane == row + 3 * rank), 1.0, 0.0)
    a = jnp.where((lane // rank) % 2 == 0, gram, ones)
    low = lane < 2 * rank
    scale = jnp.zeros((rank, 128), F32)
    for k in range(rank):
        pivot_row = a[k : k + 1, :]
        column = jnp.where(low, a[:, k : k + 1], a[:, 2 * rank + k : 2 * rank + k + 1])
        pivot = column[k : k + 1, :]
        inverse = 1.0 / pivot
        scale = jnp.where(row == k, lax.rsqrt(pivot), scale)
        a = jnp.where(row > k, a - column * (inverse * pivot_row), a)
    a = a * scale
    zero = jnp.zeros((rank, left_ref.shape[1]), F32)
    z = (own_ref[...] + near_ref[...] + by_core(t_ref, got[0:n], got[n : 2 * n])) * SCALE
    for m in range(modes):
        part = jnp.where(lane // rank == 2 * m + 1, a, 0.0)
        at = slice(m * rank, (m + 1) * rank)
        for value, ref in ((z[at], z_ref), (left_ref[at, :], b_ref)):
            stacked = [zero] * 4
            stacked[2 * m + 1] = value
            ref[at, :] = mm(part, jnp.concatenate(stacked, axis=0), NN, HIGHEST)


def solve(t, own, near, chip, got0, got1, left):
    shape = jax.ShapeDtypeStruct(left.shape, F32)
    return pl.pallas_call(
        solve_kernel,
        in_specs=[SMEM] + [VMEM] * 6,
        out_specs=[VMEM, VMEM],
        out_shape=[shape, shape],
        compiler_params=params(),
        cost_estimate=cost(10**7, 10**7),
        name="solve",
    )(t, own, near, chip, got0, got1, left)


def right_kernel(h_ref, z_ref, b_ref, x_ref, e_ref, near_ref, own_ref):
    modes = e_ref.shape[0]
    rank = z_ref.shape[0] // modes
    product = split_mm(z_ref[...], x_ref[...], NN, 2)
    parts = []
    for m in range(modes):
        at = slice(m * rank, (m + 1) * rank)
        parts.append(product[at] + split_mm(b_ref[at, :], e_ref[m], NT, 2))
    i = pl.program_id(0)

    @pl.when(i < 2)
    def _():
        near_ref[...] = jnp.concatenate(parts, axis=0)

    @pl.when(i >= 2)
    def _():
        own_ref[...] = jnp.concatenate(parts, axis=0)


def right_halves(core, bit, bit_near, z, b, x, e):
    rows, depth = x.shape
    modes, _, cols = e.shape
    chunk = depth // 4
    at, at_near = core * 2 + bit, (1 - core) * 2 + bit_near
    place = jnp.stack([at_near ^ 1, at_near, at ^ 1, at])
    shape = jax.ShapeDtypeStruct((z.shape[0], depth // 2), F32)
    return pl.pallas_call(
        right_kernel,
        grid_spec=pltpu.PrefetchScalarGridSpec(
            num_scalar_prefetch=1,
            grid=(4,),
            in_specs=[
                pl.BlockSpec(z.shape, lambda i, h: (0, 0)),
                pl.BlockSpec(b.shape, lambda i, h: (0, 0)),
                pl.BlockSpec((rows, chunk), lambda i, h: (0, h[i])),
                pl.BlockSpec((modes, chunk, cols), lambda i, h: (0, h[i], 0)),
            ],
            out_specs=[
                pl.BlockSpec((z.shape[0], chunk), lambda i, h: (0, jnp.minimum(i, 1))),
                pl.BlockSpec((z.shape[0], chunk), lambda i, h: (0, jnp.maximum(i - 2, 0))),
            ],
        ),
        out_shape=[shape, shape],
        compiler_params=params("arbitrary"),
        cost_estimate=cost(8 * depth * rows * 128, x.nbytes + e.nbytes),
        name="right",
    )(place, z, b, hbm(x), hbm(e))


def moment_kernel(t_ref, x0, x1, a0, a1, b0, b1, g_ref, e_ref, *refs):
    out_ref = refs[-1]
    modes = g_ref.shape[0]
    rows = x0.shape[0]
    low = 2 + t_ref[0] % 2
    terms = ((0, x0[...]), (1, x1[...]), (low, by_core(t_ref, a0[...], a1[...])), (low ^ 1, by_core(t_ref, b0[...], b1[...])))
    for m in range(modes):
        total = 0.0
        for j, x in terms:
            total = total + mm(x, g_ref[m, rows_of(t_ref, j, rows), :], TN)
        out_ref[m] = total * SCALE + e_ref[m].astype(F32)


def moment_quarter(quarter, t, xs, g, e, so_far=()):
    rows, depth = xs[0].shape
    modes, tokens, cols = g.shape
    chunk = depth // 8
    first = 2 * quarter
    both = pl.BlockSpec((rows, chunk), lambda i, t: (0, first + i))
    on0 = pl.BlockSpec((rows, chunk), lambda i, t: (0, (first + i) * (1 - t[0] % 2)))
    on1 = pl.BlockSpec((rows, chunk), lambda i, t: (0, (first + i) * (t[0] % 2)))
    return pl.pallas_call(
        moment_kernel,
        grid_spec=pltpu.PrefetchScalarGridSpec(
            num_scalar_prefetch=1,
            grid=(2,),
            in_specs=[
                both,
                both,
                on0,
                on1,
                on0,
                on1,
                pl.BlockSpec(g.shape, lambda i, t: (0, 0, 0)),
                pl.BlockSpec((modes, chunk, cols), lambda i, t: (0, first + i, 0)),
            ]
            + [pl.BlockSpec(memory_space=pl.ANY)] * len(so_far),
            out_specs=pl.BlockSpec((modes, chunk, cols), lambda i, t: (0, first + i, 0)),
        ),
        out_shape=pltpu.HBM((modes, depth, cols), F32),
        input_output_aliases={9: 0} if so_far else {},
        compiler_params=params("arbitrary"),
        cost_estimate=cost(2 * depth * modes * cols * tokens // 4, 8 * 2**20),
        name="moment",
    )(t, hbm(xs[0]), *xs[1:], g, hbm(e), *so_far)


def error_kernel(q_ref, m_ref, r0, r1, b_ref, *refs):
    out_ref, right_ref = refs[-2:]
    modes = out_ref.shape[0]
    rank = b_ref.shape[0] // modes
    right = jnp.where(pl.program_id(0) == 0, r0[...], r1[...])
    right_ref[...] = right.astype(F32)
    for m in range(modes):
        at = slice(m * rank, (m + 1) * rank)
        stacked = jnp.concatenate([right[at], right[at]], axis=0)
        out_ref[m] = m_ref[m] - mm(stacked, split(b_ref[at, :], 2), TN)


def error_quarters(places, moments, rights, b, so_far=(), pieces=1):
    modes, depth, cols = moments.shape
    ranks, width = rights[0].shape
    width //= pieces
    spec = pl.BlockSpec((modes, width, cols), lambda i, j, q: (0, q[i] * pieces + j, 0))
    half = pl.BlockSpec((ranks, width), lambda i, j, q: (0, j))
    return pl.pallas_call(
        error_kernel,
        grid_spec=pltpu.PrefetchScalarGridSpec(
            num_scalar_prefetch=1,
            grid=(2, pieces),
            in_specs=[spec, half, half, pl.BlockSpec(b.shape, lambda i, j, q: (0, 0))]
            + [pl.BlockSpec(memory_space=pl.ANY)] * len(so_far),
            out_specs=[spec, pl.BlockSpec((ranks, width), lambda i, j, q: (0, q[i] * pieces + j))],
        ),
        out_shape=[
            pltpu.HBM(moments.shape, F32),
            pltpu.HBM((ranks, depth), F32),
        ],
        input_output_aliases={1: 0, 5: 1} if so_far else {1: 0},
        compiler_params=params("arbitrary", "arbitrary"),
        cost_estimate=cost(10**6, 8 * 2**20),
        name="error",
    )(jnp.stack(places), moments, *rights, b, *so_far)


def grad_kernel(t_ref, g_ref, w_ref, keep_ref, send_ref):
    rows = keep_ref.shape[0] // 2
    w = jnp.concatenate([w_ref[0], w_ref[1]], axis=1)
    for j, (ref, top) in enumerate(((keep_ref, 0), (send_ref, 0), (keep_ref, rows), (send_ref, rows))):
        at = rows_of(t_ref, j, rows)
        g = jnp.concatenate([g_ref[0, at, :], g_ref[1, at, :]], axis=1)
        ref[top : top + rows, :] = mm(g, w, NT).astype(BF16)


def grad_half(half, t, g, w, chunk=1024):
    modes, depth, cols = w.shape
    rows = g.shape[1] // 2
    steps = depth // 2 // chunk
    first = half * steps
    shape = jax.ShapeDtypeStruct((rows, depth // 2), BF16)
    return pl.pallas_call(
        grad_kernel,
        grid=(steps,),
        in_specs=[
            SMEM,
            pl.BlockSpec(g.shape, lambda i: (0, 0, 0)),
            pl.BlockSpec((modes, chunk, cols), lambda i: (0, first + i, 0)),
        ],
        out_specs=[pl.BlockSpec((rows, chunk), lambda i: (0, i))] * 2,
        out_shape=[shape, shape],
        compiler_params=params("arbitrary"),
        cost_estimate=cost(4 * rows * depth * modes * cols, w.nbytes),
        name="grad",
    )(t, g, hbm(w))


def pair_kernel(sizes, a_ref, b_ref, *outs):
    total = (a_ref[...].astype(F32) + b_ref[...].astype(F32)).astype(BF16)
    chunk = total.shape[1]
    i = pl.program_id(0)
    first = 0
    for size, out in zip(sizes, outs):
        for u in range(size):

            @pl.when(i == first + u)
            def _(out=out, u=u):
                out[:, u * chunk : (u + 1) * chunk] = total

        first += size


def pair_sum(a, b, sizes):
    rows, width = a.shape
    rows //= 2
    chunk = width // sum(sizes)
    spec = pl.BlockSpec((rows, chunk), lambda i: (1, i))
    shapes = [(rows, size * chunk) for size in sizes]
    return pl.pallas_call(
        partial(pair_kernel, sizes),
        grid=(sum(sizes),),
        in_specs=[spec, spec],
        out_specs=[pl.BlockSpec(shape, lambda i: (0, 0)) for shape in shapes],
        out_shape=[jax.ShapeDtypeStruct(shape, BF16) for shape in shapes],
        compiler_params=params("arbitrary"),
        cost_estimate=cost(rows * width, 6 * rows * width),
        name="pair_sum",
    )(a, b)


def finish_kernel(a_ref, b_ref, c_ref, *refs):
    total = a_ref[...].astype(F32) + b_ref[...].astype(F32)
    refs[-1][...] = (total + c_ref[...].astype(F32)).astype(BF16)


def finish_grad(place, depth, keep, near, first, far, so_far=()):
    rows, width = far.shape
    chunk = depth // 8
    if width % (2 * chunk) == 0 and place % 2 == 0 and first % 2 == 0:
        chunk, place, first = 2 * chunk, place // 2, first // 2
    mine = pl.BlockSpec((rows, chunk), lambda i: (0, first + i))
    return pl.pallas_call(
        finish_kernel,
        grid=(width // chunk,),
        in_specs=[mine, mine, pl.BlockSpec((rows, chunk), lambda i: (0, i))]
        + [pl.BlockSpec(memory_space=pl.ANY)] * len(so_far),
        out_specs=pl.BlockSpec((rows, chunk), lambda i: (0, place + i)),
        out_shape=pltpu.HBM((rows, depth), BF16),
        input_output_aliases={3: 0} if so_far else {},
        compiler_params=params("arbitrary"),
        cost_estimate=cost(far.size, 3 * far.nbytes),
        name="finish_grad",
    )(keep, near, far, *so_far)


def compress(moments, right_prev):
    highest = lax.Precision.HIGHEST
    replicas = lax.axis_size("dp")
    projected = jnp.einsum("mdc,mrd->mrc", moments, right_prev, precision=highest)
    left_sum = lax.psum(projected, "dp")
    gram_matrix = lax.psum(
        jnp.einsum("mrc,msc->mrs", left_sum, left_sum, precision=highest), "tensor"
    )
    factor = jnp.linalg.cholesky(gram_matrix)
    ortho_basis = jax.vmap(partial(jax.scipy.linalg.solve_triangular, lower=True))(factor, left_sum)
    right_local = jnp.einsum("mdc,mrc->mrd", moments, ortho_basis, precision=highest)
    right_total = lax.psum(right_local, "tensor")
    right_total = lax.psum(right_total, "dp")
    right_mean = right_total / replicas
    approximation = jnp.einsum("mrd,mrc->mdc", right_mean, ortho_basis, precision=highest)
    return (moments - approximation, right_mean)


def any_mesh(layer_input, kv_weight, kv_cotangent, error_before, right_factor):
    portion = kv_cotangent
    weight_grad = jnp.einsum(
        "td,mtc->mdc",
        lax.all_gather(layer_input, "tensor", axis=0, tiled=True),
        portion,
        preferred_element_type=jnp.float32,
    )
    moments = weight_grad * TOKENS ** (-0.5) + error_before[0].astype(jnp.float32)
    portion = kv_cotangent
    input_sum = lax.psum_scatter(
        jnp.einsum("mtc,mdc->td", portion, kv_weight, preferred_element_type=jnp.float32).astype(
            jnp.bfloat16
        ),
        "tensor",
        scatter_dimension=0,
        tiled=True,
    )
    leading = compress(moments[0:1], right_factor[0:1])
    second = compress(moments[1:2], right_factor[1:2])
    errors = jnp.concatenate([leading[0], second[0]], axis=0)
    right_next = jnp.concatenate([leading[1], second[1]], axis=0)
    return (errors[None], right_next, input_sum)


def tie(value, *others):
    return lax.optimization_barrier((value, *others))[0]


def per_device(layer_input, kv_weight, kv_cotangent, error_before, right_factor):
    tensor, replicas = lax.axis_size("tensor"), lax.axis_size("dp")
    t = lax.axis_index("tensor").astype(jnp.int32)
    d = lax.axis_index("dp").astype(jnp.int32)
    core = t & 1
    place = t.reshape(1)
    errors = error_before[0]
    depth = layer_input.shape[1]
    n = 2 * right_factor.shape[1]
    bits = replicas.bit_length() - 1

    def swap(value):
        return lax.ppermute(value, "tensor", [(i, i ^ 1) for i in range(tensor)])

    def cross(value, carrier=None):
        cores = range(tensor) if carrier is None else range(carrier, tensor, 2)
        return lax.ppermute(value, "tensor", [(i, i ^ 2) for i in cores])

    def hop(value, step):
        pairs = []
        for i in range(replicas):
            for k in range(tensor):
                bit = (step + 1 - k % 2) % bits
                pairs.append((i * tensor + k, (i ^ (1 << bit)) * tensor + k))
        return lax.ppermute(value, ("dp", "tensor"), pairs)

    bit0, bit1 = (d >> (1 % bits)) & 1, d & 1
    bit, bit_near = jnp.where(core == 1, bit1, bit0), jnp.where(core == 1, bit0, bit1)
    at, at_near = core * 2 + bit, (1 - core) * 2 + bit_near
    places = (at, at_near, at ^ 1, at_near ^ 1)
    always = d + t < replicas + tensor

    def together(steps, *args):
        def skipped(*args):
            shapes = jax.eval_shape(steps, *args)
            return jax.tree.map(lambda v: jnp.zeros(v.shape, v.dtype), shapes)

        return lax.cond(always, steps, skipped, *args)

    xa0 = cross(layer_input, 0)

    def project_rows(x, r, errors):
        y = project(x, r)
        y_near = swap(y)
        y_far = cross(jnp.concatenate([y, y_near], axis=0), 1)
        x_near = swap(tie(x, y_near))
        e = feedback(tie(r, y_near), errors)
        y_far = tie(y_far, e, x_near)
        return (y, y_near, swap(y_far), y_far), e, x_near

    ys, e, x_near = together(project_rows, layer_input, right_factor, errors)
    xb0 = cross(x_near, 0)

    def left_factors(ys, e):
        left = left_local(place, ys, kv_cotangent, e)
        grads = []
        for k in range(bits):
            arrived = hop(left, k)
            if k < 2:
                grads.append(grad_half(k, place, kv_cotangent, tie(kv_weight, left)))
                arrived = tie(arrived, grads[k][0])
            if k == 1:
                got0 = swap(tie(grads[0][1], left))
                arrived = tie(arrived, got0)
            elif k == 2:
                got1 = swap(tie(grads[1][1], left))
                (first,) = pair_sum(grads[0][0], tie(got0, left), (2,))
                arrived = tie(arrived, first, got1)
            left = left + arrived
        return left, grads, got0, got1, first

    left, grads, got0, got1, first = together(left_factors, ys, e)
    (keep0, _), (keep1, _) = grads
    left, xa0 = lax.optimization_barrier((left, xa0))

    def spread_out(left, keep1, got1):
        own, send, far = spread(place, left, kv_cotangent)
        near = swap(jnp.concatenate([send, far], axis=0))
        chip = far + near[n:]
        got = cross(chip, 1)
        pieces = pair_sum(tie(keep1, chip), got1, SECOND_PIECES)
        got = tie(got, *pieces)
        return own, near[:n], chip, swap(got), got, pieces

    own, near, chip, *gots, (second, third) = together(spread_out, left, keep1, got1)
    chip, xb0, first = lax.optimization_barrier((chip, xb0, first))
    first = cross(first)

    def right_halves_of(own, near, chip, got0, got, left, xa0, xb0):
        xa1 = swap(xa0)
        z, b = solve(place, own, near, chip, got0, got, left)
        xb1 = swap(tie(xb0, z))
        half_near, half = right_halves(core, bit, bit_near, z, b, layer_input, errors)
        half_near = swap(tie(half_near, xa1, xb1))
        quarter = half.shape[1] // 2
        give = (half[:, :quarter] + half_near[:, :quarter]).astype(BF16)
        return b, give, half[:, quarter:] + half_near[:, quarter:], xa1, xb1

    args = (own, near, chip, *gots, left, xa0, xb0)
    b, give, own, xa1, xb1 = together(right_halves_of, *args)
    second = cross(tie(second, give))

    def moments_of(j, xs, after, *so_far):
        return moment_quarter(j, place, xs, tie(kv_cotangent, after), errors, so_far)

    xs = (layer_input, x_near, xa0, xa1, xb0, xb1)

    def right_sums(give, own, xs):
        moments = moments_of(0, xs, give)
        own = own + tie(hop(give, 0), moments).astype(F32)
        for k in range(1, bits):
            rounded = lax.optimization_barrier(own.astype(BF16))
            moments = moments_of(k, xs, rounded, moments)
            own = rounded.astype(F32) + tie(hop(rounded, k), moments).astype(F32)
        return own.astype(BF16), moments

    own, moments = together(right_sums, give, own, xs)
    own, first, second = lax.optimization_barrier((own, first, second))

    def over_x(own, keep0, got0, first, keep1, got1, second):
        arrived = cross(own)
        grad = finish_grad(0, depth, keep0, got0, 0, tie(first, own))
        grad = finish_grad(4, depth, keep1, got1, 0, second, (grad,))
        own = own.astype(F32) + tie(arrived, grad).astype(F32)
        return (own * (1.0 / replicas)).astype(BF16), grad

    own, grad = together(over_x, own, keep0, got0, first, keep1, got1, second)
    third = cross(tie(third, own))

    def first_errors(own, b, moments, xs):
        other = hop(own, 0)
        near = swap(own)
        moments = moments_of(3, xs, own, moments)
        other = tie(other, moments)
        other_near = swap(other)
        after, right = error_quarters(places[:2], moments, (own, near), b)
        return after, right, other, tie(other_near, right)

    after, right, other, other_near = together(first_errors, own, b, moments, xs)
    after, right = error_quarters(places[2:], after, (other, other_near), b, (right,))
    done = SECOND_PIECES[0]
    grad = finish_grad(4 + done, depth, keep1, got1, done, tie(third, other_near), (grad,))
    return (after[None], right.reshape(right_factor.shape), grad)


def solution(mesh):
    sizes = mesh.shape
    fits = sizes["tensor"] == 4 and sizes["dp"] == 8
    return jax.shard_map(
        per_device if fits else any_mesh,
        mesh=mesh,
        in_specs=(
            P(("dp", "tensor"), None),
            P(None, None, "tensor"),
            P(None, "dp", "tensor"),
            P("dp", None, None, "tensor"),
            P(),
        ),
        out_specs=(P("dp", None, None, "tensor"), P(), P(("dp", "tensor"), None)),
        check_vma=False,
    )
```

```python
from functools import partial

import jax
import jax.numpy as jnp
from jax import lax
from jax.experimental import pallas as pl
from jax.experimental.pallas import tpu as pltpu
from jax.sharding import PartitionSpec as P

TOKENS = 1024
SCALE = TOKENS ** (-0.5)
F32, BF16 = jnp.float32, jnp.bfloat16
WEIGHT = 4096
MOMENT_STEPS = 2
SECOND_PIECES = (6, 10)
VMEM_LIMIT = 12 * 1024 * 1024
NN = (((1,), (0,)), ((), ()))
NT = (((1,), (1,)), ((), ()))
TN = (((0,), (0,)), ((), ()))
HIGHEST = lax.Precision.HIGHEST


def mm(a, b, dims, precision=None):
    return lax.dot_general(a, b, dims, precision=precision, preferred_element_type=F32)


def split(value, terms):
    parts, rest = [], value
    for _ in range(terms):
        part = rest.astype(BF16)
        parts.append(part)
        rest = rest - part.astype(F32)
    return jnp.concatenate(parts, axis=0)


def split_mm(a, b, dims, terms):
    rows = a.shape[0]
    product = mm(split(a, terms), b, dims)
    total = product[:rows]
    for k in range(1, terms):
        total = total + product[k * rows : (k + 1) * rows]
    return total


def params(*semantics):
    return pltpu.CompilerParams(
        vmem_limit_bytes=VMEM_LIMIT,
        dimension_semantics=semantics if semantics else None,
    )


SMEM = pl.BlockSpec(memory_space=pltpu.SMEM)
VMEM = pl.BlockSpec(memory_space=pltpu.VMEM)


def hbm(value):
    return pltpu.with_memory_space_constraint(value, pltpu.HBM)


def cost(flops, nbytes):
    return pl.CostEstimate(flops=int(flops) // WEIGHT, bytes_accessed=int(nbytes) // WEIGHT, transcendentals=0)


def project_kernel(x_ref, r_ref, y_ref):
    modes, rank, chunk = r_ref.shape
    term = split_mm(r_ref[...].reshape(modes * rank, chunk), x_ref[...], NT, 3)

    @pl.when(pl.program_id(0) == 0)
    def _():
        y_ref[...] = term

    @pl.when(pl.program_id(0) > 0)
    def _():
        y_ref[...] += term


def project(x, r, chunk=2048):
    rows, depth = x.shape
    modes, rank, _ = r.shape
    return pl.pallas_call(
        project_kernel,
        grid=(depth // chunk,),
        in_specs=[
            pl.BlockSpec((rows, chunk), lambda i: (0, i)),
            pl.BlockSpec((modes, rank, chunk), lambda i: (0, 0, i)),
        ],
        out_specs=pl.BlockSpec((modes * rank, rows), lambda i: (0, 0)),
        out_shape=jax.ShapeDtypeStruct((modes * rank, rows), F32),
        compiler_params=params("arbitrary"),
        cost_estimate=cost(6 * rows * depth * modes * rank, x.nbytes + r.nbytes),
        name="project",
    )(hbm(x), hbm(r))


def feedback_kernel(r_ref, e_ref, out_ref):
    term = split_mm(r_ref[0], e_ref[0], NN, 3)

    @pl.when(pl.program_id(1) == 0)
    def _():
        out_ref[...] = term

    @pl.when(pl.program_id(1) > 0)
    def _():
        out_ref[...] += term


def feedback(r, e, chunk=2048):
    modes, rank, depth = r.shape
    cols = e.shape[-1]
    return pl.pallas_call(
        feedback_kernel,
        grid=(modes, depth // chunk),
        in_specs=[
            pl.BlockSpec((1, rank, chunk), lambda m, i: (m, 0, i)),
            pl.BlockSpec((1, chunk, cols), lambda m, i: (m, i, 0)),
        ],
        out_specs=pl.BlockSpec((rank, cols), lambda m, i: (m, 0)),
        out_shape=jax.ShapeDtypeStruct((modes * rank, cols), F32),
        compiler_params=params("arbitrary", "arbitrary"),
        cost_estimate=cost(6 * modes * rank * depth * cols, r.nbytes + e.nbytes),
        name="feedback",
    )(hbm(r), hbm(e))


def rows_of(t_ref, j, rows):
    return pl.ds(pl.multiple_of((t_ref[0] ^ j) * rows, rows), rows)


def by_core(t_ref, on_core0, on_core1):
    return jnp.where(t_ref[0] % 2 == 0, on_core0, on_core1)


def left_kernel(t_ref, own, near, far0, far1, g_ref, e_ref, out_ref):
    modes = g_ref.shape[0]
    rank, rows = own.shape[0] // modes, own.shape[1]
    n = modes * rank
    far = by_core(t_ref, far0[...], far1[...])
    same = by_core(t_ref, far[n:], far[:n])
    other = by_core(t_ref, far[:n], far[n:])
    for m in range(modes):
        at = slice(m * rank, (m + 1) * rank)
        total = 0.0
        for j, y in enumerate((own[...], near[...], same, other)):
            total = total + split_mm(y[at], g_ref[m, rows_of(t_ref, j, rows), :], NN, 3)
        out_ref[at, :] = total * SCALE + e_ref[at, :]


def left_local(t, ys, g, e):
    return pl.pallas_call(
        left_kernel,
        in_specs=[SMEM] + [VMEM] * 6,
        out_specs=VMEM,
        out_shape=jax.ShapeDtypeStruct(e.shape, F32),
        compiler_params=params(),
        cost_estimate=cost(6 * e.size * g.shape[1], g.nbytes),
        name="left",
    )(t, *ys, g, e)


def spread_kernel(t_ref, left_ref, g_ref, own_ref, near_ref, far_ref):
    modes = g_ref.shape[0]
    rank = left_ref.shape[0] // modes
    rows = own_ref.shape[1]
    n = modes * rank
    low = 2 + t_ref[0] % 2
    for j, (ref, top) in ((0, (own_ref, 0)), (1, (near_ref, 0)), (low, (far_ref, 0)), (low ^ 1, (far_ref, n))):
        for m in range(modes):
            ref[top + m * rank : top + (m + 1) * rank, :] = split_mm(
                left_ref[m * rank : (m + 1) * rank, :], g_ref[m, rows_of(t_ref, j, rows), :], NT, 3
            )
    zero = jnp.zeros((rank, left_ref.shape[1]), F32)
    a, b = left_ref[0:rank, :], left_ref[rank : 2 * rank, :]
    gram = mm(a, jnp.concatenate([a, zero, zero, zero], axis=0), NT, HIGHEST)
    gram = gram + mm(b, jnp.concatenate([zero, zero, b, zero], axis=0), NT, HIGHEST)
    far_ref[2 * n :, 0:128] = gram
    far_ref[2 * n :, 128:] = jnp.zeros((rank, rows - 128), F32)


def spread(t, left, g):
    rows = g.shape[1] // 4
    n = left.shape[0]
    small = jax.ShapeDtypeStruct((n, rows), F32)
    return pl.pallas_call(
        spread_kernel,
        in_specs=[SMEM, VMEM, VMEM],
        out_specs=[VMEM, VMEM, VMEM],
        out_shape=[small, small, jax.ShapeDtypeStruct((2 * n + n // 2, rows), F32)],
        compiler_params=params(),
        cost_estimate=cost(6 * left.size * g.shape[1], g.nbytes),
        name="spread",
    )(t, left, g)


def solve_kernel(t_ref, own_ref, near_ref, chip_ref, got0, got1, left_ref, z_ref, b_ref):
    modes = 2
    rank = left_ref.shape[0] // modes
    n = modes * rank
    got = by_core(t_ref, got0[...], got1[...])
    gram = chip_ref[2 * n :, 0:128] + got[2 * n :, 0:128]
    row = lax.broadcasted_iota(jnp.int32, (rank, 128), 0)
    lane = lax.broadcasted_iota(jnp.int32, (rank, 128), 1)
    ones = jnp.where((lane == row + rank) | (lane == row + 3 * rank), 1.0, 0.0)
    a = jnp.where((lane // rank) % 2 == 0, gram, ones)
    low = lane < 2 * rank
    scale = jnp.zeros((rank, 128), F32)
    for k in range(rank):
        pivot_row = a[k : k + 1, :]
        column = jnp.where(low, a[:, k : k + 1], a[:, 2 * rank + k : 2 * rank + k + 1])
        pivot = column[k : k + 1, :]
        inverse = 1.0 / pivot
        scale = jnp.where(row == k, lax.rsqrt(pivot), scale)
        a = jnp.where(row > k, a - column * (inverse * pivot_row), a)
    a = a * scale
    zero = jnp.zeros((rank, left_ref.shape[1]), F32)
    z = (own_ref[...] + near_ref[...] + by_core(t_ref, got[0:n], got[n : 2 * n])) * SCALE
    for m in range(modes):
        part = jnp.where(lane // rank == 2 * m + 1, a, 0.0)
        at = slice(m * rank, (m + 1) * rank)
        for value, ref in ((z[at], z_ref), (left_ref[at, :], b_ref)):
            stacked = [zero] * 4
            stacked[2 * m + 1] = value
            ref[at, :] = mm(part, jnp.concatenate(stacked, axis=0), NN, HIGHEST)


def solve(t, own, near, chip, got0, got1, left):
    shape = jax.ShapeDtypeStruct(left.shape, F32)
    return pl.pallas_call(
        solve_kernel,
        in_specs=[SMEM] + [VMEM] * 6,
        out_specs=[VMEM, VMEM],
        out_shape=[shape, shape],
        compiler_params=params(),
        cost_estimate=cost(10**7, 10**7),
        name="solve",
    )(t, own, near, chip, got0, got1, left)


def right_kernel(h_ref, z_ref, b_ref, x_ref, e_ref, near_ref, own_ref):
    modes, width, _ = e_ref.shape
    rank = z_ref.shape[0] // modes
    product = split_mm(z_ref[...], x_ref[...], NN, 2)
    parts = []
    for m in range(modes):
        at = slice(m * rank, (m + 1) * rank)
        parts.append(product[at] + split_mm(b_ref[at, :], e_ref[m], NT, 2))
    whole = jnp.concatenate(parts, axis=0)
    low, high = whole[:, : width // 2], whole[:, width // 2 :]
    i = pl.program_id(0)
    keep_high = h_ref[2 + i] == 1
    ordered = jnp.concatenate([jnp.where(keep_high, low, high), jnp.where(keep_high, high, low)], axis=1)

    @pl.when(i == 0)
    def _():
        near_ref[...] = ordered

    @pl.when(i == 1)
    def _():
        own_ref[...] = ordered


def right_halves(core, bit, bit_near, z, b, x, e):
    rows, depth = x.shape
    modes, _, cols = e.shape
    width = depth // 2
    shape = jax.ShapeDtypeStruct((z.shape[0], width), F32)
    whole = pl.BlockSpec(shape.shape, lambda i, h: (0, 0))
    return pl.pallas_call(
        right_kernel,
        grid_spec=pltpu.PrefetchScalarGridSpec(
            num_scalar_prefetch=1,
            grid=(2,),
            in_specs=[
                pl.BlockSpec(z.shape, lambda i, h: (0, 0)),
                pl.BlockSpec(b.shape, lambda i, h: (0, 0)),
                pl.BlockSpec((rows, width), lambda i, h: (0, h[i])),
                pl.BlockSpec((modes, width, cols), lambda i, h: (0, h[i], 0)),
            ],
            out_specs=[whole, whole],
        ),
        out_shape=[shape, shape],
        compiler_params=params("arbitrary"),
        cost_estimate=cost(8 * depth * rows * 128, x.nbytes + e.nbytes),
        name="right",
    )(jnp.stack([1 - core, core, bit_near, bit]), z, b, hbm(x), hbm(e))


def moment_kernel(t_ref, x0, x1, a0, a1, b0, b1, g_ref, e_ref, *refs):
    out_ref = refs[-1]
    modes = g_ref.shape[0]
    rows = x0.shape[0]
    low = 2 + t_ref[0] % 2
    terms = ((0, x0[...]), (1, x1[...]), (low, by_core(t_ref, a0[...], a1[...])), (low ^ 1, by_core(t_ref, b0[...], b1[...])))
    for m in range(modes):
        total = 0.0
        for j, x in terms:
            total = total + mm(x, g_ref[m, rows_of(t_ref, j, rows), :], TN)
        out_ref[m] = total * SCALE + e_ref[m].astype(F32)


def moment_quarter(quarter, t, xs, g, e, so_far=()):
    rows, depth = xs[0].shape
    modes, tokens, cols = g.shape
    steps = MOMENT_STEPS
    chunk = depth // 4 // steps
    first = steps * quarter
    both = pl.BlockSpec((rows, chunk), lambda i, t: (0, first + i))
    on0 = pl.BlockSpec((rows, chunk), lambda i, t: (0, (first + i) * (1 - t[0] % 2)))
    on1 = pl.BlockSpec((rows, chunk), lambda i, t: (0, (first + i) * (t[0] % 2)))
    return pl.pallas_call(
        moment_kernel,
        grid_spec=pltpu.PrefetchScalarGridSpec(
            num_scalar_prefetch=1,
            grid=(steps,),
            in_specs=[
                both,
                both,
                on0,
                on1,
                on0,
                on1,
                pl.BlockSpec(g.shape, lambda i, t: (0, 0, 0)),
                pl.BlockSpec((modes, chunk, cols), lambda i, t: (0, first + i, 0)),
            ]
            + [pl.BlockSpec(memory_space=pl.ANY)] * len(so_far),
            out_specs=pl.BlockSpec((modes, chunk, cols), lambda i, t: (0, first + i, 0)),
        ),
        out_shape=pltpu.HBM((modes, depth, cols), F32),
        input_output_aliases={9: 0} if so_far else {},
        compiler_params=params("arbitrary"),
        cost_estimate=cost(2 * depth * modes * cols * tokens // 4, 8 * 2**20),
        name="moment",
    )(t, *xs, g, hbm(e), *so_far)


def error_kernel(q_ref, m_ref, r0, r1, b_ref, *refs):
    out_ref, right_ref = refs[-2:]
    modes = out_ref.shape[0]
    rank = b_ref.shape[0] // modes
    right = jnp.where(pl.program_id(0) == 0, r0[...], r1[...])
    right_ref[...] = right.astype(F32)
    for m in range(modes):
        at = slice(m * rank, (m + 1) * rank)
        stacked = jnp.concatenate([right[at], right[at]], axis=0)
        out_ref[m] = m_ref[m] - mm(stacked, split(b_ref[at, :], 2), TN)


def error_quarters(places, moments, rights, b, so_far=(), pieces=1):
    modes, depth, cols = moments.shape
    ranks, width = rights[0].shape
    width //= pieces
    spec = pl.BlockSpec((modes, width, cols), lambda i, j, q: (0, q[i] * pieces + j, 0))
    half = pl.BlockSpec((ranks, width), lambda i, j, q: (0, j))
    return pl.pallas_call(
        error_kernel,
        grid_spec=pltpu.PrefetchScalarGridSpec(
            num_scalar_prefetch=1,
            grid=(2, pieces),
            in_specs=[spec, half, half, pl.BlockSpec(b.shape, lambda i, j, q: (0, 0))]
            + [pl.BlockSpec(memory_space=pl.ANY)] * len(so_far),
            out_specs=[spec, pl.BlockSpec((ranks, width), lambda i, j, q: (0, q[i] * pieces + j))],
        ),
        out_shape=[
            pltpu.HBM(moments.shape, F32),
            pltpu.HBM((ranks, depth), F32),
        ],
        input_output_aliases={1: 0, 5: 1} if so_far else {1: 0},
        compiler_params=params("arbitrary", "arbitrary"),
        cost_estimate=cost(10**6, 8 * 2**20),
        name="error",
    )(jnp.stack(places), moments, *rights, b, *so_far)


def grad_kernel(t_ref, g_ref, w_ref, keep_ref, send_ref):
    rows = keep_ref.shape[0] // 2
    w = jnp.concatenate([w_ref[0], w_ref[1]], axis=1)
    for j, (ref, top) in enumerate(((keep_ref, 0), (send_ref, 0), (keep_ref, rows), (send_ref, rows))):
        at = rows_of(t_ref, j, rows)
        g = jnp.concatenate([g_ref[0, at, :], g_ref[1, at, :]], axis=1)
        ref[top : top + rows, :] = mm(g, w, NT).astype(BF16)


def grad_half(half, t, g, w, chunk=1024):
    modes, depth, cols = w.shape
    rows = g.shape[1] // 2
    steps = depth // 2 // chunk
    first = half * steps
    shape = jax.ShapeDtypeStruct((rows, depth // 2), BF16)
    return pl.pallas_call(
        grad_kernel,
        grid=(steps,),
        in_specs=[
            SMEM,
            pl.BlockSpec(g.shape, lambda i: (0, 0, 0)),
            pl.BlockSpec((modes, chunk, cols), lambda i: (0, first + i, 0)),
        ],
        out_specs=[pl.BlockSpec((rows, chunk), lambda i: (0, i))] * 2,
        out_shape=[shape, shape],
        compiler_params=params("arbitrary"),
        cost_estimate=cost(4 * rows * depth * modes * cols, w.nbytes),
        name="grad",
    )(t, g, hbm(w))


def pair_kernel(a0, b0, a1, b1, own_ref, *outs):
    own_ref[...] = (a0[...].astype(F32) + b0[...].astype(F32)).astype(BF16)
    total = (a1[...].astype(F32) + b1[...].astype(F32)).astype(BF16)
    first = 0
    for out in outs:
        out[...] = total[:, first : first + out.shape[1]]
        first += out.shape[1]


def pair_sum(a, b, sizes, steps=2):
    rows, width = a.shape
    rows //= 2
    widths = [width] + [width * size // sum(sizes) for size in sizes]
    own = pl.BlockSpec((rows // steps, width), lambda i: (i, 0))
    far = pl.BlockSpec((rows // steps, width), lambda i: (steps + i, 0))
    return pl.pallas_call(
        pair_kernel,
        grid=(steps,),
        in_specs=[own, own, far, far],
        out_specs=[pl.BlockSpec((rows // steps, w), lambda i: (i, 0)) for w in widths],
        out_shape=[jax.ShapeDtypeStruct((rows, w), BF16) for w in widths],
        compiler_params=params("arbitrary"),
        cost_estimate=cost(2 * rows * width, 12 * rows * width),
        name="pair_sum",
    )(a, b, a, b)


def finish_kernel(count, own_ref, *refs):
    out_ref = refs[-1]
    first = 0
    for far_ref in refs[:count]:
        at = slice(first, first + far_ref.shape[1])
        out_ref[:, at] = (own_ref[:, at].astype(F32) + far_ref[...].astype(F32)).astype(BF16)
        first = at.stop


def finish_grad(half, own, fars, so_far=(), steps=2):
    rows, width = own.shape
    return pl.pallas_call(
        partial(finish_kernel, len(fars)),
        grid=(steps,),
        in_specs=[pl.BlockSpec((rows // steps, width), lambda i: (i, 0))]
        + [pl.BlockSpec((rows // steps, far.shape[1]), lambda i: (i, 0)) for far in fars]
        + [pl.BlockSpec(memory_space=pl.ANY)] * len(so_far),
        out_specs=pl.BlockSpec((rows // steps, width), lambda i: (i, half)),
        out_shape=pltpu.HBM((rows, 2 * width), BF16),
        input_output_aliases={1 + len(fars): 0} if so_far else {},
        compiler_params=params("arbitrary"),
        cost_estimate=cost(3 * rows * width, 8 * rows * width),
        name="finish_grad",
    )(own, *fars, *so_far)


def compress(moments, right_prev):
    highest = lax.Precision.HIGHEST
    replicas = lax.axis_size("dp")
    projected = jnp.einsum("mdc,mrd->mrc", moments, right_prev, precision=highest)
    left_sum = lax.psum(projected, "dp")
    gram_matrix = lax.psum(
        jnp.einsum("mrc,msc->mrs", left_sum, left_sum, precision=highest), "tensor"
    )
    factor = jnp.linalg.cholesky(gram_matrix)
    ortho_basis = jax.vmap(partial(jax.scipy.linalg.solve_triangular, lower=True))(factor, left_sum)
    right_local = jnp.einsum("mdc,mrc->mrd", moments, ortho_basis, precision=highest)
    right_total = lax.psum(right_local, "tensor")
    right_total = lax.psum(right_total, "dp")
    right_mean = right_total / replicas
    approximation = jnp.einsum("mrd,mrc->mdc", right_mean, ortho_basis, precision=highest)
    return (moments - approximation, right_mean)


def any_mesh(layer_input, kv_weight, kv_cotangent, error_before, right_factor):
    portion = kv_cotangent
    weight_grad = jnp.einsum(
        "td,mtc->mdc",
        lax.all_gather(layer_input, "tensor", axis=0, tiled=True),
        portion,
        preferred_element_type=jnp.float32,
    )
    moments = weight_grad * TOKENS ** (-0.5) + error_before[0].astype(jnp.float32)
    portion = kv_cotangent
    input_sum = lax.psum_scatter(
        jnp.einsum("mtc,mdc->td", portion, kv_weight, preferred_element_type=jnp.float32).astype(
            jnp.bfloat16
        ),
        "tensor",
        scatter_dimension=0,
        tiled=True,
    )
    leading = compress(moments[0:1], right_factor[0:1])
    second = compress(moments[1:2], right_factor[1:2])
    errors = jnp.concatenate([leading[0], second[0]], axis=0)
    right_next = jnp.concatenate([leading[1], second[1]], axis=0)
    return (errors[None], right_next, input_sum)


def tie(value, *others):
    return lax.optimization_barrier((value, *others))[0]


def per_device(layer_input, kv_weight, kv_cotangent, error_before, right_factor):
    tensor, replicas = lax.axis_size("tensor"), lax.axis_size("dp")
    t = lax.axis_index("tensor").astype(jnp.int32)
    d = lax.axis_index("dp").astype(jnp.int32)
    core = t & 1
    place = t.reshape(1)
    errors = error_before[0]
    depth = layer_input.shape[1]
    n = 2 * right_factor.shape[1]
    bits = replicas.bit_length() - 1

    def swap(value):
        return lax.ppermute(value, "tensor", [(i, i ^ 1) for i in range(tensor)])

    def cross(value, carrier=None):
        cores = range(tensor) if carrier is None else range(carrier, tensor, 2)
        return lax.ppermute(value, "tensor", [(i, i ^ 2) for i in cores])

    def hop(value, step):
        pairs = []
        for i in range(replicas):
            for k in range(tensor):
                bit = (step + 1 - k % 2) % bits
                pairs.append((i * tensor + k, (i ^ (1 << bit)) * tensor + k))
        return lax.ppermute(value, ("dp", "tensor"), pairs)

    bit0, bit1 = (d >> (1 % bits)) & 1, d & 1
    bit, bit_near = jnp.where(core == 1, bit1, bit0), jnp.where(core == 1, bit0, bit1)
    at, at_near = core * 2 + bit, (1 - core) * 2 + bit_near
    places = (at, at_near, at ^ 1, at_near ^ 1)
    always = d + t < replicas + tensor

    def together(steps, *args):
        def skipped(*args):
            shapes = jax.eval_shape(steps, *args)
            return jax.tree.map(lambda v: jnp.zeros(v.shape, v.dtype), shapes)

        return lax.cond(always, steps, skipped, *args)

    xa0 = cross(layer_input, 0)

    def project_rows(x, r):
        x_near = swap(x)
        y = project(tie(x, r), r)
        y_near = swap(y)
        return x_near, y, y_near, jnp.concatenate([y, y_near], axis=0)

    x_near, y, y_near, pair = together(project_rows, layer_input, right_factor)

    def exchange(pair, r, errors):
        y_far = cross(pair, 1)
        e = feedback(tie(r, pair), errors)
        return tie(y_far, e), e

    y_far, e = together(exchange, pair, right_factor, errors)
    xb0 = cross(tie(x_near, y_far), 0)

    def left_factors(y, y_near, y_far, e):
        left = left_local(place, (y, y_near, swap(y_far), y_far), kv_cotangent, e)
        grads = []
        for k in range(bits):
            arrived = hop(left, k)
            if k < 2:
                grads.append(grad_half(k, place, kv_cotangent, tie(kv_weight, left)))
                arrived = tie(arrived, grads[k][0])
            if k == 1:
                got0 = swap(tie(grads[0][1], left))
                arrived = tie(arrived, got0)
            elif k == 2:
                got1 = swap(tie(grads[1][1], left))
                own0, first = pair_sum(grads[0][0], tie(got0, left), (1,))
                arrived = tie(arrived, first, got1)
            left = left + arrived
        return left, grads[1][0], got1, own0, first

    left, keep1, got1, own0, first = together(left_factors, y, y_near, y_far, e)
    left, xa0 = lax.optimization_barrier((left, xa0))

    def spread_out(left, keep1, got1, xa0):
        own, send, far = spread(place, left, kv_cotangent)
        near = swap(jnp.concatenate([send, far], axis=0))
        chip = far + near[n:]
        got = cross(chip, 1)
        xa1 = swap(tie(xa0, chip))
        own1, *pieces = pair_sum(tie(keep1, chip), got1, SECOND_PIECES)
        got = tie(got, xa1, own1, *pieces)
        return own, near[:n], chip, swap(got), got, own1, pieces, xa1

    own, near, chip, *gots, own1, (second, third), xa1 = together(spread_out, left, keep1, got1, xa0)
    first = cross(tie(first, chip))
    chip, xb0 = lax.optimization_barrier((chip, xb0))

    def right_halves_of(own, near, chip, got0, got, left, xb0):
        xb1 = swap(xb0)
        z, b = solve(place, own, near, chip, got0, got, left)
        half_near, half = right_halves(core, bit, bit_near, z, b, layer_input, errors)
        half_near = swap(tie(half_near, xb1))
        quarter = half.shape[1] // 2
        give = (half[:, :quarter] + half_near[:, :quarter]).astype(BF16)
        return b, give, half[:, quarter:] + half_near[:, quarter:], xb1

    args = (own, near, chip, *gots, left, xb0)
    b, give, own, xb1 = together(right_halves_of, *args)
    second = cross(tie(second, give))

    def moments_of(j, xs, after, *so_far):
        return moment_quarter(j, place, xs, tie(kv_cotangent, after), errors, so_far)

    xs = (layer_input, x_near, xa0, xa1, xb0, xb1)

    def right_sums(give, own, xs):
        moments = moments_of(0, xs, give)
        own = own + tie(hop(give, 0), moments).astype(F32)
        for k in range(1, bits):
            rounded = lax.optimization_barrier(own.astype(BF16))
            moments = moments_of(k, xs, rounded, moments)
            own = rounded.astype(F32) + tie(hop(rounded, k), moments).astype(F32)
        return own.astype(BF16), moments

    own, moments = together(right_sums, give, own, xs)
    own, first, second = lax.optimization_barrier((own, first, second))

    def last_quarters(own, third, b, moments, xs, own0, first):
        arrived = cross(own)
        moments = moments_of(3, xs, own, moments)
        own = own.astype(F32) + tie(arrived, moments).astype(F32)
        own = lax.optimization_barrier((own * (1.0 / replicas)).astype(BF16))
        third = cross(tie(third, own))
        other = hop(own, 0)
        near = swap(own)
        after, right = error_quarters(places[:2], moments, (own, near), b)
        other = tie(other, right)
        other_near = swap(other)
        grad = finish_grad(0, own0, (tie(first, other),))
        other_near = tie(other_near, grad)
        return *error_quarters(places[2:], after, (other, other_near), b, (right,)), grad, third

    after, right, grad, third = together(last_quarters, own, third, b, moments, xs, own0, first)
    grad = finish_grad(1, own1, (second, third), (grad,))
    return (after[None], right.reshape(right_factor.shape), grad)


def solution(mesh):
    sizes = mesh.shape
    fits = sizes["tensor"] == 4 and sizes["dp"] == 8
    return jax.shard_map(
        per_device if fits else any_mesh,
        mesh=mesh,
        in_specs=(
            P(("dp", "tensor"), None),
            P(None, None, "tensor"),
            P(None, "dp", "tensor"),
            P("dp", None, None, "tensor"),
            P(),
        ),
        out_specs=(P("dp", None, None, "tensor"), P(), P(("dp", "tensor"), None)),
        check_vma=False,
    )
```

```python
from functools import partial

import jax
import jax.numpy as jnp
from jax import lax
from jax.experimental import pallas as pl
from jax.experimental.pallas import tpu as pltpu
from jax.sharding import PartitionSpec as P

TOKENS = 1024
SCALE = TOKENS ** (-0.5)
F32, BF16 = jnp.float32, jnp.bfloat16
WEIGHT = 4096
MOMENT_STEPS = 2
SECOND_PIECES = (6, 10)
VMEM_LIMIT = 12 * 1024 * 1024
NN = (((1,), (0,)), ((), ()))
NT = (((1,), (1,)), ((), ()))
TN = (((0,), (0,)), ((), ()))
HIGHEST = lax.Precision.HIGHEST


def mm(a, b, dims, precision=None):
    return lax.dot_general(a, b, dims, precision=precision, preferred_element_type=F32)


def split(value, terms):
    parts, rest = [], value
    for _ in range(terms):
        part = rest.astype(BF16)
        parts.append(part)
        rest = rest - part.astype(F32)
    return jnp.concatenate(parts, axis=0)


def split_mm(a, b, dims, terms):
    rows = a.shape[0]
    product = mm(split(a, terms), b, dims)
    total = product[:rows]
    for k in range(1, terms):
        total = total + product[k * rows : (k + 1) * rows]
    return total


def params(*semantics):
    return pltpu.CompilerParams(
        vmem_limit_bytes=VMEM_LIMIT,
        dimension_semantics=semantics if semantics else None,
    )


SMEM = pl.BlockSpec(memory_space=pltpu.SMEM)
VMEM = pl.BlockSpec(memory_space=pltpu.VMEM)


def vmem(value):
    return pltpu.with_memory_space_constraint(value, pltpu.VMEM)


def hbm(value):
    return pltpu.with_memory_space_constraint(value, pltpu.HBM)


def cost(flops, nbytes):
    return pl.CostEstimate(flops=int(flops) // WEIGHT, bytes_accessed=int(nbytes) // WEIGHT, transcendentals=0)


def project_kernel(x_ref, r_ref, y_ref):
    modes, rank, chunk = r_ref.shape
    term = split_mm(r_ref[...].reshape(modes * rank, chunk), x_ref[...], NT, 3)

    @pl.when(pl.program_id(0) == 0)
    def _():
        y_ref[...] = term

    @pl.when(pl.program_id(0) > 0)
    def _():
        y_ref[...] += term


def project(x, r, chunk=2048):
    rows, depth = x.shape
    modes, rank, _ = r.shape
    return pl.pallas_call(
        project_kernel,
        grid=(depth // chunk,),
        in_specs=[
            pl.BlockSpec((rows, chunk), lambda i: (0, i)),
            pl.BlockSpec((modes, rank, chunk), lambda i: (0, 0, i)),
        ],
        out_specs=pl.BlockSpec((modes * rank, rows), lambda i: (0, 0)),
        out_shape=jax.ShapeDtypeStruct((modes * rank, rows), F32),
        compiler_params=params("arbitrary"),
        cost_estimate=cost(6 * rows * depth * modes * rank, x.nbytes + r.nbytes),
        name="project",
    )(hbm(x), hbm(r))


def feedback_kernel(r_ref, e_ref, out_ref):
    term = split_mm(r_ref[0], e_ref[0], NN, 3)

    @pl.when(pl.program_id(1) == 0)
    def _():
        out_ref[...] = term

    @pl.when(pl.program_id(1) > 0)
    def _():
        out_ref[...] += term


def feedback(r, e, chunk=2048):
    modes, rank, depth = r.shape
    cols = e.shape[-1]
    return pl.pallas_call(
        feedback_kernel,
        grid=(modes, depth // chunk),
        in_specs=[
            pl.BlockSpec((1, rank, chunk), lambda m, i: (m, 0, i)),
            pl.BlockSpec((1, chunk, cols), lambda m, i: (m, i, 0)),
        ],
        out_specs=pl.BlockSpec((rank, cols), lambda m, i: (m, 0)),
        out_shape=jax.ShapeDtypeStruct((modes * rank, cols), F32),
        compiler_params=params("arbitrary", "arbitrary"),
        cost_estimate=cost(6 * modes * rank * depth * cols, r.nbytes + e.nbytes),
        name="feedback",
    )(hbm(r), hbm(e))


def rows_of(t_ref, j, rows):
    return pl.ds(pl.multiple_of((t_ref[0] ^ j) * rows, rows), rows)


def by_core(t_ref, on_core0, on_core1):
    return jnp.where(t_ref[0] % 2 == 0, on_core0, on_core1)


def left_kernel(t_ref, own, near, far0, far1, g_ref, e_ref, out_ref):
    modes = g_ref.shape[0]
    rank, rows = own.shape[0] // modes, own.shape[1]
    n = modes * rank
    far = by_core(t_ref, far0[...], far1[...])
    same = by_core(t_ref, far[n:], far[:n])
    other = by_core(t_ref, far[:n], far[n:])
    for m in range(modes):
        at = slice(m * rank, (m + 1) * rank)
        total = 0.0
        for j, y in enumerate((own[...], near[...], same, other)):
            total = total + split_mm(y[at], g_ref[m, rows_of(t_ref, j, rows), :], NN, 3)
        out_ref[at, :] = total * SCALE + e_ref[at, :]


def left_local(t, ys, g, e):
    return pl.pallas_call(
        left_kernel,
        in_specs=[SMEM] + [VMEM] * 6,
        out_specs=VMEM,
        out_shape=jax.ShapeDtypeStruct(e.shape, F32),
        compiler_params=params(),
        cost_estimate=cost(6 * e.size * g.shape[1], g.nbytes),
        name="left",
    )(t, *ys, g, e)


def spread_kernel(t_ref, left_ref, g_ref, own_ref, near_ref, far_ref):
    modes = g_ref.shape[0]
    rank = left_ref.shape[0] // modes
    rows = own_ref.shape[1]
    n = modes * rank
    low = 2 + t_ref[0] % 2
    for j, (ref, top) in ((0, (own_ref, 0)), (1, (near_ref, 0)), (low, (far_ref, 0)), (low ^ 1, (far_ref, n))):
        for m in range(modes):
            ref[top + m * rank : top + (m + 1) * rank, :] = split_mm(
                left_ref[m * rank : (m + 1) * rank, :], g_ref[m, rows_of(t_ref, j, rows), :], NT, 3
            )
    zero = jnp.zeros((rank, left_ref.shape[1]), F32)
    a, b = left_ref[0:rank, :], left_ref[rank : 2 * rank, :]
    gram = mm(a, jnp.concatenate([a, zero, zero, zero], axis=0), NT, HIGHEST)
    gram = gram + mm(b, jnp.concatenate([zero, zero, b, zero], axis=0), NT, HIGHEST)
    far_ref[2 * n :, 0:128] = gram
    far_ref[2 * n :, 128:] = jnp.zeros((rank, rows - 128), F32)


def spread(t, left, g):
    rows = g.shape[1] // 4
    n = left.shape[0]
    small = jax.ShapeDtypeStruct((n, rows), F32)
    return pl.pallas_call(
        spread_kernel,
        in_specs=[SMEM, VMEM, VMEM],
        out_specs=[VMEM, VMEM, VMEM],
        out_shape=[small, small, jax.ShapeDtypeStruct((2 * n + n // 2, rows), F32)],
        compiler_params=params(),
        cost_estimate=cost(6 * left.size * g.shape[1], g.nbytes),
        name="spread",
    )(t, left, g)


def solve_kernel(t_ref, own_ref, near_ref, chip_ref, got0, got1, left_ref, z_ref, b_ref):
    modes = 2
    rank = left_ref.shape[0] // modes
    n = modes * rank
    got = by_core(t_ref, got0[...], got1[...])
    gram = chip_ref[2 * n :, 0:128] + got[2 * n :, 0:128]
    row = lax.broadcasted_iota(jnp.int32, (rank, 128), 0)
    lane = lax.broadcasted_iota(jnp.int32, (rank, 128), 1)
    ones = jnp.where((lane == row + rank) | (lane == row + 3 * rank), 1.0, 0.0)
    a = jnp.where((lane // rank) % 2 == 0, gram, ones)
    low = lane < 2 * rank
    scale = jnp.zeros((rank, 128), F32)
    for k in range(rank):
        pivot_row = a[k : k + 1, :]
        column = jnp.where(low, a[:, k : k + 1], a[:, 2 * rank + k : 2 * rank + k + 1])
        pivot = column[k : k + 1, :]
        inverse = 1.0 / pivot
        scale = jnp.where(row == k, lax.rsqrt(pivot), scale)
        a = jnp.where(row > k, a - column * (inverse * pivot_row), a)
    a = a * scale
    zero = jnp.zeros((rank, left_ref.shape[1]), F32)
    z = (own_ref[...] + near_ref[0:n, :] + by_core(t_ref, got[0:n], got[n : 2 * n])) * SCALE
    for m in range(modes):
        part = jnp.where(lane // rank == 2 * m + 1, a, 0.0)
        at = slice(m * rank, (m + 1) * rank)
        for value, ref in ((z[at], z_ref), (left_ref[at, :], b_ref)):
            stacked = [zero] * 4
            stacked[2 * m + 1] = value
            ref[at, :] = mm(part, jnp.concatenate(stacked, axis=0), NN, HIGHEST)


def solve(t, own, near, chip, got0, got1, left):
    shape = jax.ShapeDtypeStruct(left.shape, F32)
    return pl.pallas_call(
        solve_kernel,
        in_specs=[SMEM] + [VMEM] * 6,
        out_specs=[VMEM, VMEM],
        out_shape=[shape, shape],
        compiler_params=params(),
        cost_estimate=cost(10**7, 10**7),
        name="solve",
    )(t, own, near, chip, got0, got1, left)


def right_kernel(h_ref, z_ref, b_ref, x_ref, e_ref, near_ref, own_ref):
    modes, width, _ = e_ref.shape
    rank = z_ref.shape[0] // modes
    product = split_mm(z_ref[...], x_ref[...], NN, 2)
    parts = []
    for m in range(modes):
        at = slice(m * rank, (m + 1) * rank)
        parts.append(product[at] + split_mm(b_ref[at, :], e_ref[m], NT, 2))
    whole = jnp.concatenate(parts, axis=0)
    low, high = whole[:, : width // 2], whole[:, width // 2 :]
    i = pl.program_id(0)
    keep_high = h_ref[2 + i] == 1
    ordered = jnp.concatenate([jnp.where(keep_high, low, high), jnp.where(keep_high, high, low)], axis=1)

    @pl.when(i == 0)
    def _():
        near_ref[...] = ordered

    @pl.when(i == 1)
    def _():
        own_ref[...] = ordered


def right_halves(core, bit, bit_near, z, b, x, e):
    rows, depth = x.shape
    modes, _, cols = e.shape
    width = depth // 2
    shape = jax.ShapeDtypeStruct((z.shape[0], width), F32)
    whole = pl.BlockSpec(shape.shape, lambda i, h: (0, 0))
    return pl.pallas_call(
        right_kernel,
        grid_spec=pltpu.PrefetchScalarGridSpec(
            num_scalar_prefetch=1,
            grid=(2,),
            in_specs=[
                pl.BlockSpec(z.shape, lambda i, h: (0, 0)),
                pl.BlockSpec(b.shape, lambda i, h: (0, 0)),
                pl.BlockSpec((rows, width), lambda i, h: (0, h[i])),
                pl.BlockSpec((modes, width, cols), lambda i, h: (0, h[i], 0)),
            ],
            out_specs=[whole, whole],
        ),
        out_shape=[shape, shape],
        compiler_params=params("arbitrary"),
        cost_estimate=cost(8 * depth * rows * 128, x.nbytes + e.nbytes),
        name="right",
    )(jnp.stack([1 - core, core, bit_near, bit]), z, b, hbm(x), hbm(e))


def moment_kernel(t_ref, x0, x1, a0, a1, b0, b1, g_ref, e_ref, *refs):
    out_ref = refs[-1]
    modes = g_ref.shape[0]
    rows = x0.shape[0]
    low = 2 + t_ref[0] % 2
    terms = ((0, x0[...]), (1, x1[...]), (low, by_core(t_ref, a0[...], a1[...])), (low ^ 1, by_core(t_ref, b0[...], b1[...])))
    for m in range(modes):
        total = 0.0
        for j, x in terms:
            total = total + mm(x, g_ref[m, rows_of(t_ref, j, rows), :], TN)
        out_ref[m] = total * SCALE + e_ref[m].astype(F32)


def moment_quarter(quarter, t, xs, g, e, so_far=()):
    rows, depth = xs[0].shape
    modes, tokens, cols = g.shape
    steps = MOMENT_STEPS
    chunk = depth // 4 // steps
    first = steps * quarter
    both = pl.BlockSpec((rows, chunk), lambda i, t: (0, first + i))
    on0 = pl.BlockSpec((rows, chunk), lambda i, t: (0, (first + i) * (1 - t[0] % 2)))
    on1 = pl.BlockSpec((rows, chunk), lambda i, t: (0, (first + i) * (t[0] % 2)))
    return pl.pallas_call(
        moment_kernel,
        grid_spec=pltpu.PrefetchScalarGridSpec(
            num_scalar_prefetch=1,
            grid=(steps,),
            in_specs=[
                both,
                both,
                on0,
                on1,
                on0,
                on1,
                pl.BlockSpec(g.shape, lambda i, t: (0, 0, 0)),
                pl.BlockSpec((modes, chunk, cols), lambda i, t: (0, first + i, 0)),
            ]
            + [pl.BlockSpec(memory_space=pl.ANY)] * len(so_far),
            out_specs=pl.BlockSpec((modes, chunk, cols), lambda i, t: (0, first + i, 0)),
        ),
        out_shape=pltpu.HBM((modes, depth, cols), F32),
        input_output_aliases={9: 0} if so_far else {},
        compiler_params=params("arbitrary"),
        cost_estimate=cost(2 * depth * modes * cols * tokens // 4, 8 * 2**20),
        name="moment",
    )(t, *xs, g, hbm(e), *so_far)


def error_kernel(q_ref, m_ref, r0, r1, b_ref, *refs):
    out_ref, right_ref = refs[-2:]
    modes = out_ref.shape[0]
    rank = b_ref.shape[0] // modes
    right = jnp.where(pl.program_id(0) == 0, r0[...], r1[...])
    right_ref[...] = right.astype(F32)
    for m in range(modes):
        at = slice(m * rank, (m + 1) * rank)
        stacked = jnp.concatenate([right[at], right[at]], axis=0)
        out_ref[m] = m_ref[m] - mm(stacked, split(b_ref[at, :], 2), TN)


def error_quarters(places, moments, rights, b, so_far=(), pieces=1):
    modes, depth, cols = moments.shape
    ranks, width = rights[0].shape
    width //= pieces
    spec = pl.BlockSpec((modes, width, cols), lambda i, j, q: (0, q[i] * pieces + j, 0))
    half = pl.BlockSpec((ranks, width), lambda i, j, q: (0, j))
    return pl.pallas_call(
        error_kernel,
        grid_spec=pltpu.PrefetchScalarGridSpec(
            num_scalar_prefetch=1,
            grid=(2, pieces),
            in_specs=[spec, half, half, pl.BlockSpec(b.shape, lambda i, j, q: (0, 0))]
            + [pl.BlockSpec(memory_space=pl.ANY)] * len(so_far),
            out_specs=[spec, pl.BlockSpec((ranks, width), lambda i, j, q: (0, q[i] * pieces + j))],
        ),
        out_shape=[
            pltpu.HBM(moments.shape, F32),
            pltpu.HBM((ranks, depth), F32),
        ],
        input_output_aliases={1: 0, 5: 1} if so_far else {1: 0},
        compiler_params=params("arbitrary", "arbitrary"),
        cost_estimate=cost(10**6, 8 * 2**20),
        name="error",
    )(jnp.stack(places), moments, *rights, b, *so_far)


def grad_kernel(t_ref, g_ref, w_ref, keep_ref, send_ref):
    rows = keep_ref.shape[0] // 2
    w = jnp.concatenate([w_ref[0], w_ref[1]], axis=1)
    for j, (ref, top) in enumerate(((keep_ref, 0), (send_ref, 0), (keep_ref, rows), (send_ref, rows))):
        at = rows_of(t_ref, j, rows)
        g = jnp.concatenate([g_ref[0, at, :], g_ref[1, at, :]], axis=1)
        ref[top : top + rows, :] = mm(g, w, NT).astype(BF16)


def grad_half(half, t, g, w, chunk=1024):
    modes, depth, cols = w.shape
    rows = g.shape[1] // 2
    steps = depth // 2 // chunk
    first = half * steps
    shape = jax.ShapeDtypeStruct((rows, depth // 2), BF16)
    return pl.pallas_call(
        grad_kernel,
        grid=(steps,),
        in_specs=[
            SMEM,
            pl.BlockSpec(g.shape, lambda i: (0, 0, 0)),
            pl.BlockSpec((modes, chunk, cols), lambda i: (0, first + i, 0)),
        ],
        out_specs=[pl.BlockSpec((rows, chunk), lambda i: (0, i))] * 2,
        out_shape=[shape, shape],
        compiler_params=params("arbitrary"),
        cost_estimate=cost(4 * rows * depth * modes * cols, w.nbytes),
        name="grad",
    )(t, g, hbm(w))


def pair_kernel(a0, b0, a1, b1, own_ref, *outs):
    own_ref[...] = (a0[...].astype(F32) + b0[...].astype(F32)).astype(BF16)
    total = (a1[...].astype(F32) + b1[...].astype(F32)).astype(BF16)
    first = 0
    for out in outs:
        out[...] = total[:, first : first + out.shape[1]]
        first += out.shape[1]


def pair_sum(a, b, sizes, steps=2):
    rows, width = a.shape
    rows //= 2
    widths = [width] + [width * size // sum(sizes) for size in sizes]
    own = pl.BlockSpec((rows // steps, width), lambda i: (i, 0))
    far = pl.BlockSpec((rows // steps, width), lambda i: (steps + i, 0))
    return pl.pallas_call(
        pair_kernel,
        grid=(steps,),
        in_specs=[own, own, far, far],
        out_specs=[pl.BlockSpec((rows // steps, w), lambda i: (i, 0)) for w in widths],
        out_shape=[jax.ShapeDtypeStruct((rows, w), BF16) for w in widths],
        compiler_params=params("arbitrary"),
        cost_estimate=cost(2 * rows * width, 12 * rows * width),
        name="pair_sum",
    )(a, b, a, b)


def finish_kernel(count, own_ref, *refs):
    out_ref = refs[-1]
    first = 0
    for far_ref in refs[:count]:
        at = slice(first, first + far_ref.shape[1])
        out_ref[:, at] = (own_ref[:, at].astype(F32) + far_ref[...].astype(F32)).astype(BF16)
        first = at.stop


def finish_grad(half, own, fars, so_far=(), steps=2):
    rows, width = own.shape
    return pl.pallas_call(
        partial(finish_kernel, len(fars)),
        grid=(steps,),
        in_specs=[pl.BlockSpec((rows // steps, width), lambda i: (i, 0))]
        + [pl.BlockSpec((rows // steps, far.shape[1]), lambda i: (i, 0)) for far in fars]
        + [pl.BlockSpec(memory_space=pl.ANY)] * len(so_far),
        out_specs=pl.BlockSpec((rows // steps, width), lambda i: (i, half)),
        out_shape=pltpu.HBM((rows, 2 * width), BF16),
        input_output_aliases={1 + len(fars): 0} if so_far else {},
        compiler_params=params("arbitrary"),
        cost_estimate=cost(3 * rows * width, 8 * rows * width),
        name="finish_grad",
    )(own, *fars, *so_far)


def compress(moments, right_prev):
    highest = lax.Precision.HIGHEST
    replicas = lax.axis_size("dp")
    projected = jnp.einsum("mdc,mrd->mrc", moments, right_prev, precision=highest)
    left_sum = lax.psum(projected, "dp")
    gram_matrix = lax.psum(
        jnp.einsum("mrc,msc->mrs", left_sum, left_sum, precision=highest), "tensor"
    )
    factor = jnp.linalg.cholesky(gram_matrix)
    ortho_basis = jax.vmap(partial(jax.scipy.linalg.solve_triangular, lower=True))(factor, left_sum)
    right_local = jnp.einsum("mdc,mrc->mrd", moments, ortho_basis, precision=highest)
    right_total = lax.psum(right_local, "tensor")
    right_total = lax.psum(right_total, "dp")
    right_mean = right_total / replicas
    approximation = jnp.einsum("mrd,mrc->mdc", right_mean, ortho_basis, precision=highest)
    return (moments - approximation, right_mean)


def any_mesh(layer_input, kv_weight, kv_cotangent, error_before, right_factor):
    portion = kv_cotangent
    weight_grad = jnp.einsum(
        "td,mtc->mdc",
        lax.all_gather(layer_input, "tensor", axis=0, tiled=True),
        portion,
        preferred_element_type=jnp.float32,
    )
    moments = weight_grad * TOKENS ** (-0.5) + error_before[0].astype(jnp.float32)
    portion = kv_cotangent
    input_sum = lax.psum_scatter(
        jnp.einsum("mtc,mdc->td", portion, kv_weight, preferred_element_type=jnp.float32).astype(
            jnp.bfloat16
        ),
        "tensor",
        scatter_dimension=0,
        tiled=True,
    )
    leading = compress(moments[0:1], right_factor[0:1])
    second = compress(moments[1:2], right_factor[1:2])
    errors = jnp.concatenate([leading[0], second[0]], axis=0)
    right_next = jnp.concatenate([leading[1], second[1]], axis=0)
    return (errors[None], right_next, input_sum)


def tie(value, *others):
    return lax.optimization_barrier((value, *others))[0]


def per_device(layer_input, kv_weight, kv_cotangent, error_before, right_factor):
    tensor, replicas = lax.axis_size("tensor"), lax.axis_size("dp")
    t = lax.axis_index("tensor").astype(jnp.int32)
    d = lax.axis_index("dp").astype(jnp.int32)
    core = t & 1
    place = t.reshape(1)
    errors = error_before[0]
    depth = layer_input.shape[1]
    n = 2 * right_factor.shape[1]
    bits = replicas.bit_length() - 1

    def swap(value):
        return lax.ppermute(value, "tensor", [(i, i ^ 1) for i in range(tensor)])

    def cross(value, carrier=None):
        cores = range(tensor) if carrier is None else range(carrier, tensor, 2)
        return lax.ppermute(value, "tensor", [(i, i ^ 2) for i in cores])

    def hop(value, step):
        pairs = []
        for i in range(replicas):
            for k in range(tensor):
                bit = (step + 1 - k % 2) % bits
                pairs.append((i * tensor + k, (i ^ (1 << bit)) * tensor + k))
        return lax.ppermute(value, ("dp", "tensor"), pairs)

    bit0, bit1 = (d >> (1 % bits)) & 1, d & 1
    bit, bit_near = jnp.where(core == 1, bit1, bit0), jnp.where(core == 1, bit0, bit1)
    at, at_near = core * 2 + bit, (1 - core) * 2 + bit_near
    places = (at, at_near, at ^ 1, at_near ^ 1)
    always = d + t < replicas + tensor

    def together(steps, *args):
        def skipped(*args):
            shapes = jax.eval_shape(steps, *args)
            return jax.tree.map(lambda v: jnp.zeros(v.shape, v.dtype), shapes)

        return lax.cond(always, steps, skipped, *args)

    xa0 = cross(layer_input, 0)

    def project_rows(x, r):
        x_near = swap(x)
        y = project(tie(x, r), r)
        y_near = swap(y)
        return x_near, y, y_near, jnp.concatenate([y, y_near], axis=0)

    x_near, y, y_near, pair = together(project_rows, layer_input, right_factor)

    def exchange(pair, r, errors):
        y_far = cross(pair, 1)
        e = feedback(tie(r, pair), errors)
        return tie(y_far, e), e

    y_far, e = together(exchange, pair, right_factor, errors)
    xb0 = cross(tie(x_near, y_far), 0)

    def left_factors(y, y_near, y_far, e):
        left = left_local(place, (y, y_near, swap(y_far), y_far), kv_cotangent, e)
        grads = []
        for k in range(bits):
            arrived = hop(left, k)
            if k < 2:
                grads.append(grad_half(k, place, kv_cotangent, tie(kv_weight, left)))
                arrived = tie(arrived, grads[k][0])
            if k == 1:
                got0 = swap(tie(grads[0][1], left))
                arrived = tie(arrived, got0)
            elif k == 2:
                got1 = swap(tie(grads[1][1], left))
                own0, first = pair_sum(grads[0][0], tie(got0, left), (1,))
                arrived = tie(arrived, first, got1)
            left = left + arrived
        return left, grads[1][0], got1, own0, first

    left, keep1, got1, own0, first = together(left_factors, y, y_near, y_far, e)
    left, xa0 = lax.optimization_barrier((left, xa0))

    def spread_out(left, keep1, got1, xa0):
        own, send, far = spread(place, left, kv_cotangent)
        near = swap(jnp.concatenate([send, far], axis=0))
        chip = far + near[n:]
        got = cross(chip, 1)
        xa1 = swap(tie(xa0, chip))
        own1, *pieces = pair_sum(tie(keep1, chip), got1, SECOND_PIECES)
        got = tie(got, xa1, own1, *pieces)
        return own, near[:n], chip, swap(got), got, own1, pieces, xa1

    own, near, chip, *gots, own1, (second, third), xa1 = together(spread_out, left, keep1, got1, xa0)
    first = cross(tie(first, chip))
    second = cross(tie(second, chip))
    chip, xb0 = lax.optimization_barrier((chip, xb0))

    def moments_of(j, xs, after, *so_far):
        return moment_quarter(j, place, xs, tie(kv_cotangent, after), errors, so_far)

    def right_sums(own, near, chip, got0, got, left, x_near, xa0, xa1, xb0):
        xb1 = swap(xb0)
        z, b = solve(place, own, near, chip, got0, got, left)
        half_near, half = right_halves(core, bit, bit_near, z, b, layer_input, errors)
        half_near = swap(tie(half_near, xb1))
        quarter = half.shape[1] // 2
        give = (half[:, :quarter] + half_near[:, :quarter]).astype(BF16)
        xs = (layer_input, x_near, xa0, xa1, xb0, xb1)
        moments = moments_of(0, xs, give)
        own = half[:, quarter:] + half_near[:, quarter:] + tie(hop(give, 0), moments).astype(F32)
        for k in range(1, bits):
            rounded = lax.optimization_barrier(own.astype(BF16))
            moments = moments_of(k, xs, rounded, moments)
            own = rounded.astype(F32) + tie(hop(rounded, k), moments).astype(F32)
        return own.astype(BF16), b, moments, xb1

    args = (own, near, chip, *gots, left, x_near, xa0, xa1, xb0)
    own, b, moments, xb1 = together(right_sums, *args)
    xs = (layer_input, x_near, xa0, xa1, xb0, xb1)
    own, first, second = lax.optimization_barrier((own, first, second))

    def last_quarters(own, third, b, moments, xs, own0, first):
        arrived = cross(own)
        moments = moments_of(3, xs, own, moments)
        own = own.astype(F32) + tie(arrived, moments).astype(F32)
        own = lax.optimization_barrier((own * (1.0 / replicas)).astype(BF16))
        third = cross(tie(third, own))
        other = hop(own, 0)
        near = swap(own)
        after, right = error_quarters(places[:2], moments, (own, near), b)
        other = tie(other, right)
        other_near = swap(other)
        grad = finish_grad(0, own0, (tie(first, other),))
        other_near = tie(other_near, grad)
        return *error_quarters(places[2:], after, (other, other_near), b, (right,)), grad, third

    after, right, grad, third = together(last_quarters, own, third, b, moments, xs, own0, first)
    grad = finish_grad(1, vmem(own1), (vmem(second), third), (grad,))
    return (after[None], right.reshape(right_factor.shape), grad)


def solution(mesh):
    sizes = mesh.shape
    fits = sizes["tensor"] == 4 and sizes["dp"] == 8
    return jax.shard_map(
        per_device if fits else any_mesh,
        mesh=mesh,
        in_specs=(
            P(("dp", "tensor"), None),
            P(None, None, "tensor"),
            P(None, "dp", "tensor"),
            P("dp", None, None, "tensor"),
            P(),
        ),
        out_specs=(P("dp", None, None, "tensor"), P(), P(("dp", "tensor"), None)),
        check_vma=False,
    )
```

```python
from functools import partial

import jax
import jax.numpy as jnp
from jax import lax
from jax.experimental import pallas as pl
from jax.experimental.pallas import tpu as pltpu
from jax.sharding import PartitionSpec as P

TOKENS = 1024
SCALE = TOKENS ** (-0.5)
F32, BF16 = jnp.float32, jnp.bfloat16
WEIGHT = 4096
MOMENT_STEPS = 2
SECOND_PIECES = (6, 10)
VMEM_LIMIT = 12 * 1024 * 1024
NN = (((1,), (0,)), ((), ()))
NT = (((1,), (1,)), ((), ()))
TN = (((0,), (0,)), ((), ()))
HIGHEST = lax.Precision.HIGHEST


def mm(a, b, dims, precision=None):
    return lax.dot_general(a, b, dims, precision=precision, preferred_element_type=F32)


def split(value, terms):
    parts, rest = [], value
    for _ in range(terms):
        part = rest.astype(BF16)
        parts.append(part)
        rest = rest - part.astype(F32)
    return jnp.concatenate(parts, axis=0)


def split_mm(a, b, dims, terms):
    rows = a.shape[0]
    product = mm(split(a, terms), b, dims)
    total = product[:rows]
    for k in range(1, terms):
        total = total + product[k * rows : (k + 1) * rows]
    return total


def params(*semantics):
    return pltpu.CompilerParams(
        vmem_limit_bytes=VMEM_LIMIT,
        dimension_semantics=semantics if semantics else None,
    )


SMEM = pl.BlockSpec(memory_space=pltpu.SMEM)
VMEM = pl.BlockSpec(memory_space=pltpu.VMEM)


def vmem(value):
    return pltpu.with_memory_space_constraint(value, pltpu.VMEM)


def hbm(value):
    return pltpu.with_memory_space_constraint(value, pltpu.HBM)


def cost(flops, nbytes):
    return pl.CostEstimate(flops=int(flops) // WEIGHT, bytes_accessed=int(nbytes) // WEIGHT, transcendentals=0)


def project_kernel(x_ref, r_ref, y_ref):
    modes, rank, chunk = r_ref.shape
    term = split_mm(r_ref[...].reshape(modes * rank, chunk), x_ref[...], NT, 3)

    @pl.when(pl.program_id(0) == 0)
    def _():
        y_ref[...] = term

    @pl.when(pl.program_id(0) > 0)
    def _():
        y_ref[...] += term


def project(x, r, chunk=2048):
    rows, depth = x.shape
    modes, rank, _ = r.shape
    return pl.pallas_call(
        project_kernel,
        grid=(depth // chunk,),
        in_specs=[
            pl.BlockSpec((rows, chunk), lambda i: (0, i)),
            pl.BlockSpec((modes, rank, chunk), lambda i: (0, 0, i)),
        ],
        out_specs=pl.BlockSpec((modes * rank, rows), lambda i: (0, 0)),
        out_shape=jax.ShapeDtypeStruct((modes * rank, rows), F32),
        compiler_params=params("arbitrary"),
        cost_estimate=cost(6 * rows * depth * modes * rank, x.nbytes + r.nbytes),
        name="project",
    )(hbm(x), hbm(r))


def feedback_kernel(r_ref, e_ref, out_ref):
    term = split_mm(r_ref[0], e_ref[0], NN, 3)

    @pl.when(pl.program_id(1) == 0)
    def _():
        out_ref[...] = term

    @pl.when(pl.program_id(1) > 0)
    def _():
        out_ref[...] += term


def feedback(r, e, chunk=2048):
    modes, rank, depth = r.shape
    cols = e.shape[-1]
    return pl.pallas_call(
        feedback_kernel,
        grid=(modes, depth // chunk),
        in_specs=[
            pl.BlockSpec((1, rank, chunk), lambda m, i: (m, 0, i)),
            pl.BlockSpec((1, chunk, cols), lambda m, i: (m, i, 0)),
        ],
        out_specs=pl.BlockSpec((rank, cols), lambda m, i: (m, 0)),
        out_shape=jax.ShapeDtypeStruct((modes * rank, cols), F32),
        compiler_params=params("arbitrary", "arbitrary"),
        cost_estimate=cost(6 * modes * rank * depth * cols, r.nbytes + e.nbytes),
        name="feedback",
    )(hbm(r), hbm(e))


def rows_of(t_ref, j, rows):
    return pl.ds(pl.multiple_of((t_ref[0] ^ j) * rows, rows), rows)


def by_core(t_ref, on_core0, on_core1):
    return jnp.where(t_ref[0] % 2 == 0, on_core0, on_core1)


def left_kernel(t_ref, own, near, far0, far1, g_ref, e_ref, out_ref):
    modes = g_ref.shape[0]
    rank, rows = own.shape[0] // modes, own.shape[1]
    n = modes * rank
    far = by_core(t_ref, far0[...], far1[...])
    same = by_core(t_ref, far[n:], far[:n])
    other = by_core(t_ref, far[:n], far[n:])
    for m in range(modes):
        at = slice(m * rank, (m + 1) * rank)
        total = 0.0
        for j, y in enumerate((own[...], near[...], same, other)):
            total = total + split_mm(y[at], g_ref[m, rows_of(t_ref, j, rows), :], NN, 3)
        out_ref[at, :] = total * SCALE + e_ref[at, :]


def left_local(t, ys, g, e):
    return pl.pallas_call(
        left_kernel,
        in_specs=[SMEM] + [VMEM] * 6,
        out_specs=VMEM,
        out_shape=jax.ShapeDtypeStruct(e.shape, F32),
        compiler_params=params(),
        cost_estimate=cost(6 * e.size * g.shape[1], g.nbytes),
        name="left",
    )(t, *ys, g, e)


def spread_kernel(t_ref, left_ref, g_ref, own_ref, near_ref, far_ref):
    modes = g_ref.shape[0]
    rank = left_ref.shape[0] // modes
    rows = own_ref.shape[1]
    n = modes * rank
    low = 2 + t_ref[0] % 2
    for j, (ref, top) in ((0, (own_ref, 0)), (1, (near_ref, 0)), (low, (far_ref, 0)), (low ^ 1, (far_ref, n))):
        for m in range(modes):
            ref[top + m * rank : top + (m + 1) * rank, :] = split_mm(
                left_ref[m * rank : (m + 1) * rank, :], g_ref[m, rows_of(t_ref, j, rows), :], NT, 3
            )
    zero = jnp.zeros((rank, left_ref.shape[1]), F32)
    a, b = left_ref[0:rank, :], left_ref[rank : 2 * rank, :]
    gram = mm(a, jnp.concatenate([a, zero, zero, zero], axis=0), NT, HIGHEST)
    gram = gram + mm(b, jnp.concatenate([zero, zero, b, zero], axis=0), NT, HIGHEST)
    far_ref[2 * n :, 0:128] = gram[: rank // 2]
    far_ref[2 * n :, 128:] = gram[rank // 2 :]


def spread(t, left, g):
    rows = g.shape[1] // 4
    n = left.shape[0]
    small = jax.ShapeDtypeStruct((n, rows), F32)
    return pl.pallas_call(
        spread_kernel,
        in_specs=[SMEM, VMEM, VMEM],
        out_specs=[VMEM, VMEM, VMEM],
        out_shape=[small, small, jax.ShapeDtypeStruct((2 * n + n // 4, rows), F32)],
        compiler_params=params(),
        cost_estimate=cost(6 * left.size * g.shape[1], g.nbytes),
        name="spread",
    )(t, left, g)


def solve_kernel(t_ref, own_ref, near_ref, chip_ref, got0, got1, left_ref, z_ref, b_ref):
    modes = 2
    rank = left_ref.shape[0] // modes
    n = modes * rank
    got = by_core(t_ref, got0[...], got1[...])
    gram = chip_ref[2 * n :, :] + got[2 * n :, :]
    gram = jnp.concatenate([gram[:, 0:128], gram[:, 128:]], axis=0)
    row = lax.broadcasted_iota(jnp.int32, (rank, 128), 0)
    lane = lax.broadcasted_iota(jnp.int32, (rank, 128), 1)
    ones = jnp.where((lane == row + rank) | (lane == row + 3 * rank), 1.0, 0.0)
    a = jnp.where((lane // rank) % 2 == 0, gram, ones)
    low = lane < 2 * rank
    scale = jnp.zeros((rank, 128), F32)
    for k in range(rank):
        pivot_row = a[k : k + 1, :]
        column = jnp.where(low, a[:, k : k + 1], a[:, 2 * rank + k : 2 * rank + k + 1])
        pivot = column[k : k + 1, :]
        inverse = 1.0 / pivot
        scale = jnp.where(row == k, lax.rsqrt(pivot), scale)
        a = jnp.where(row > k, a - column * (inverse * pivot_row), a)
    a = a * scale
    zero = jnp.zeros((rank, left_ref.shape[1]), F32)
    z = (own_ref[...] + near_ref[0:n, :] + by_core(t_ref, got[0:n], got[n : 2 * n])) * SCALE
    for m in range(modes):
        part = jnp.where(lane // rank == 2 * m + 1, a, 0.0)
        at = slice(m * rank, (m + 1) * rank)
        for value, ref in ((z[at], z_ref), (left_ref[at, :], b_ref)):
            stacked = [zero] * 4
            stacked[2 * m + 1] = value
            ref[at, :] = mm(part, jnp.concatenate(stacked, axis=0), NN, HIGHEST)


def solve(t, own, near, chip, got0, got1, left):
    shape = jax.ShapeDtypeStruct(left.shape, F32)
    return pl.pallas_call(
        solve_kernel,
        in_specs=[SMEM] + [VMEM] * 6,
        out_specs=[VMEM, VMEM],
        out_shape=[shape, shape],
        compiler_params=params(),
        cost_estimate=cost(10**7, 10**7),
        name="solve",
    )(t, own, near, chip, got0, got1, left)


def right_kernel(h_ref, z_ref, b_ref, x_ref, e_ref, near_ref, own_ref):
    modes, width, _ = e_ref.shape
    rank = z_ref.shape[0] // modes
    product = split_mm(z_ref[...], x_ref[...], NN, 2)
    parts = []
    for m in range(modes):
        at = slice(m * rank, (m + 1) * rank)
        parts.append(product[at] + split_mm(b_ref[at, :], e_ref[m], NT, 2))
    whole = jnp.concatenate(parts, axis=0)
    low, high = whole[:, : width // 2], whole[:, width // 2 :]
    i = pl.program_id(0)
    keep_high = h_ref[2 + i] == 1
    ordered = jnp.concatenate([jnp.where(keep_high, low, high), jnp.where(keep_high, high, low)], axis=1)

    @pl.when(i == 0)
    def _():
        near_ref[...] = ordered

    @pl.when(i == 1)
    def _():
        own_ref[...] = ordered


def right_halves(core, bit, bit_near, z, b, x, e):
    rows, depth = x.shape
    modes, _, cols = e.shape
    width = depth // 2
    shape = jax.ShapeDtypeStruct((z.shape[0], width), F32)
    whole = pl.BlockSpec(shape.shape, lambda i, h: (0, 0))
    return pl.pallas_call(
        right_kernel,
        grid_spec=pltpu.PrefetchScalarGridSpec(
            num_scalar_prefetch=1,
            grid=(2,),
            in_specs=[
                pl.BlockSpec(z.shape, lambda i, h: (0, 0)),
                pl.BlockSpec(b.shape, lambda i, h: (0, 0)),
                pl.BlockSpec((rows, width), lambda i, h: (0, h[i])),
                pl.BlockSpec((modes, width, cols), lambda i, h: (0, h[i], 0)),
            ],
            out_specs=[whole, whole],
        ),
        out_shape=[shape, shape],
        compiler_params=params("arbitrary"),
        cost_estimate=cost(8 * depth * rows * 128, x.nbytes + e.nbytes),
        name="right",
    )(jnp.stack([1 - core, core, bit_near, bit]), z, b, hbm(x), hbm(e))


def moment_kernel(t_ref, x0, x1, a0, a1, b0, b1, g_ref, e_ref, *refs):
    out_ref = refs[-1]
    modes = g_ref.shape[0]
    rows = x0.shape[0]
    low = 2 + t_ref[0] % 2
    terms = ((0, x0[...]), (1, x1[...]), (low, by_core(t_ref, a0[...], a1[...])), (low ^ 1, by_core(t_ref, b0[...], b1[...])))
    for m in range(modes):
        total = 0.0
        for j, x in terms:
            total = total + mm(x, g_ref[m, rows_of(t_ref, j, rows), :], TN)
        out_ref[m] = total * SCALE + e_ref[m].astype(F32)


def moment_quarter(quarter, t, xs, g, e, so_far=()):
    rows, depth = xs[0].shape
    modes, tokens, cols = g.shape
    steps = MOMENT_STEPS
    chunk = depth // 4 // steps
    first = steps * quarter
    both = pl.BlockSpec((rows, chunk), lambda i, t: (0, first + i))
    on0 = pl.BlockSpec((rows, chunk), lambda i, t: (0, (first + i) * (1 - t[0] % 2)))
    on1 = pl.BlockSpec((rows, chunk), lambda i, t: (0, (first + i) * (t[0] % 2)))
    return pl.pallas_call(
        moment_kernel,
        grid_spec=pltpu.PrefetchScalarGridSpec(
            num_scalar_prefetch=1,
            grid=(steps,),
            in_specs=[
                both,
                both,
                on0,
                on1,
                on0,
                on1,
                pl.BlockSpec(g.shape, lambda i, t: (0, 0, 0)),
                pl.BlockSpec((modes, chunk, cols), lambda i, t: (0, first + i, 0)),
            ]
            + [pl.BlockSpec(memory_space=pl.ANY)] * len(so_far),
            out_specs=pl.BlockSpec((modes, chunk, cols), lambda i, t: (0, first + i, 0)),
        ),
        out_shape=pltpu.HBM((modes, depth, cols), F32),
        input_output_aliases={9: 0} if so_far else {},
        compiler_params=params("arbitrary"),
        cost_estimate=cost(2 * depth * modes * cols * tokens // 4, 8 * 2**20),
        name="moment",
    )(t, *xs, g, hbm(e), *so_far)


def error_kernel(q_ref, m_ref, r0, r1, b_ref, *refs):
    out_ref, right_ref = refs[-2:]
    modes = out_ref.shape[0]
    rank = b_ref.shape[0] // modes
    right = jnp.where(pl.program_id(0) == 0, r0[...], r1[...])
    right_ref[...] = right.astype(F32)
    for m in range(modes):
        at = slice(m * rank, (m + 1) * rank)
        stacked = jnp.concatenate([right[at], right[at]], axis=0)
        out_ref[m] = m_ref[m] - mm(stacked, split(b_ref[at, :], 2), TN)


def error_quarters(places, moments, rights, b, so_far=(), pieces=1):
    modes, depth, cols = moments.shape
    ranks, width = rights[0].shape
    width //= pieces
    spec = pl.BlockSpec((modes, width, cols), lambda i, j, q: (0, q[i] * pieces + j, 0))
    half = pl.BlockSpec((ranks, width), lambda i, j, q: (0, j))
    return pl.pallas_call(
        error_kernel,
        grid_spec=pltpu.PrefetchScalarGridSpec(
            num_scalar_prefetch=1,
            grid=(2, pieces),
            in_specs=[spec, half, half, pl.BlockSpec(b.shape, lambda i, j, q: (0, 0))]
            + [pl.BlockSpec(memory_space=pl.ANY)] * len(so_far),
            out_specs=[spec, pl.BlockSpec((ranks, width), lambda i, j, q: (0, q[i] * pieces + j))],
        ),
        out_shape=[
            pltpu.HBM(moments.shape, F32),
            pltpu.HBM((ranks, depth), F32),
        ],
        input_output_aliases={1: 0, 5: 1} if so_far else {1: 0},
        compiler_params=params("arbitrary", "arbitrary"),
        cost_estimate=cost(10**6, 8 * 2**20),
        name="error",
    )(jnp.stack(places), moments, *rights, b, *so_far)


def grad_kernel(t_ref, g_ref, w_ref, keep_ref, send_ref):
    rows = keep_ref.shape[0] // 2
    w = jnp.concatenate([w_ref[0], w_ref[1]], axis=1)
    for j, (ref, top) in enumerate(((keep_ref, 0), (send_ref, 0), (keep_ref, rows), (send_ref, rows))):
        at = rows_of(t_ref, j, rows)
        g = jnp.concatenate([g_ref[0, at, :], g_ref[1, at, :]], axis=1)
        ref[top : top + rows, :] = mm(g, w, NT).astype(BF16)


def grad_half(half, t, g, w, chunk=1024):
    modes, depth, cols = w.shape
    rows = g.shape[1] // 2
    steps = depth // 2 // chunk
    first = half * steps
    shape = jax.ShapeDtypeStruct((rows, depth // 2), BF16)
    return pl.pallas_call(
        grad_kernel,
        grid=(steps,),
        in_specs=[
            SMEM,
            pl.BlockSpec(g.shape, lambda i: (0, 0, 0)),
            pl.BlockSpec((modes, chunk, cols), lambda i: (0, first + i, 0)),
        ],
        out_specs=[pl.BlockSpec((rows, chunk), lambda i: (0, i))] * 2,
        out_shape=[shape, shape],
        compiler_params=params("arbitrary"),
        cost_estimate=cost(4 * rows * depth * modes * cols, w.nbytes),
        name="grad",
    )(t, g, hbm(w))


def pair_kernel(a0, b0, a1, b1, own_ref, *outs):
    own_ref[...] = (a0[...].astype(F32) + b0[...].astype(F32)).astype(BF16)
    total = (a1[...].astype(F32) + b1[...].astype(F32)).astype(BF16)
    first = 0
    for out in outs:
        out[...] = total[:, first : first + out.shape[1]]
        first += out.shape[1]


def pair_sum(a, b, sizes, steps=2):
    rows, width = a.shape
    rows //= 2
    widths = [width] + [width * size // sum(sizes) for size in sizes]
    own = pl.BlockSpec((rows // steps, width), lambda i: (i, 0))
    far = pl.BlockSpec((rows // steps, width), lambda i: (steps + i, 0))
    return pl.pallas_call(
        pair_kernel,
        grid=(steps,),
        in_specs=[own, own, far, far],
        out_specs=[pl.BlockSpec((rows // steps, w), lambda i: (i, 0)) for w in widths],
        out_shape=[jax.ShapeDtypeStruct((rows, w), BF16) for w in widths],
        compiler_params=params("arbitrary"),
        cost_estimate=cost(2 * rows * width, 12 * rows * width),
        name="pair_sum",
    )(a, b, a, b)


def finish_kernel(count, own_ref, *refs):
    out_ref = refs[-1]
    first = 0
    for far_ref in refs[:count]:
        at = slice(first, first + far_ref.shape[1])
        out_ref[:, at] = (own_ref[:, at].astype(F32) + far_ref[...].astype(F32)).astype(BF16)
        first = at.stop


def finish_grad(half, own, fars, so_far=(), steps=2):
    rows, width = own.shape
    return pl.pallas_call(
        partial(finish_kernel, len(fars)),
        grid=(steps,),
        in_specs=[pl.BlockSpec((rows // steps, width), lambda i: (i, 0))]
        + [pl.BlockSpec((rows // steps, far.shape[1]), lambda i: (i, 0)) for far in fars]
        + [pl.BlockSpec(memory_space=pl.ANY)] * len(so_far),
        out_specs=pl.BlockSpec((rows // steps, width), lambda i: (i, half)),
        out_shape=pltpu.HBM((rows, 2 * width), BF16),
        input_output_aliases={1 + len(fars): 0} if so_far else {},
        compiler_params=params("arbitrary"),
        cost_estimate=cost(3 * rows * width, 8 * rows * width),
        name="finish_grad",
    )(own, *fars, *so_far)


def compress(moments, right_prev):
    highest = lax.Precision.HIGHEST
    replicas = lax.axis_size("dp")
    projected = jnp.einsum("mdc,mrd->mrc", moments, right_prev, precision=highest)
    left_sum = lax.psum(projected, "dp")
    gram_matrix = lax.psum(
        jnp.einsum("mrc,msc->mrs", left_sum, left_sum, precision=highest), "tensor"
    )
    factor = jnp.linalg.cholesky(gram_matrix)
    ortho_basis = jax.vmap(partial(jax.scipy.linalg.solve_triangular, lower=True))(factor, left_sum)
    right_local = jnp.einsum("mdc,mrc->mrd", moments, ortho_basis, precision=highest)
    right_total = lax.psum(right_local, "tensor")
    right_total = lax.psum(right_total, "dp")
    right_mean = right_total / replicas
    approximation = jnp.einsum("mrd,mrc->mdc", right_mean, ortho_basis, precision=highest)
    return (moments - approximation, right_mean)


def any_mesh(layer_input, kv_weight, kv_cotangent, error_before, right_factor):
    portion = kv_cotangent
    weight_grad = jnp.einsum(
        "td,mtc->mdc",
        lax.all_gather(layer_input, "tensor", axis=0, tiled=True),
        portion,
        preferred_element_type=jnp.float32,
    )
    moments = weight_grad * TOKENS ** (-0.5) + error_before[0].astype(jnp.float32)
    portion = kv_cotangent
    input_sum = lax.psum_scatter(
        jnp.einsum("mtc,mdc->td", portion, kv_weight, preferred_element_type=jnp.float32).astype(
            jnp.bfloat16
        ),
        "tensor",
        scatter_dimension=0,
        tiled=True,
    )
    leading = compress(moments[0:1], right_factor[0:1])
    second = compress(moments[1:2], right_factor[1:2])
    errors = jnp.concatenate([leading[0], second[0]], axis=0)
    right_next = jnp.concatenate([leading[1], second[1]], axis=0)
    return (errors[None], right_next, input_sum)


def tie(value, *others):
    return lax.optimization_barrier((value, *others))[0]


def per_device(layer_input, kv_weight, kv_cotangent, error_before, right_factor):
    tensor, replicas = lax.axis_size("tensor"), lax.axis_size("dp")
    t = lax.axis_index("tensor").astype(jnp.int32)
    d = lax.axis_index("dp").astype(jnp.int32)
    core = t & 1
    place = t.reshape(1)
    errors = error_before[0]
    depth = layer_input.shape[1]
    n = 2 * right_factor.shape[1]
    bits = replicas.bit_length() - 1

    def swap(value):
        return lax.ppermute(value, "tensor", [(i, i ^ 1) for i in range(tensor)])

    def cross(value, carrier=None):
        cores = range(tensor) if carrier is None else range(carrier, tensor, 2)
        return lax.ppermute(value, "tensor", [(i, i ^ 2) for i in cores])

    def hop(value, step):
        pairs = []
        for i in range(replicas):
            for k in range(tensor):
                bit = (step + 1 - k % 2) % bits
                pairs.append((i * tensor + k, (i ^ (1 << bit)) * tensor + k))
        return lax.ppermute(value, ("dp", "tensor"), pairs)

    bit0, bit1 = (d >> (1 % bits)) & 1, d & 1
    bit, bit_near = jnp.where(core == 1, bit1, bit0), jnp.where(core == 1, bit0, bit1)
    at, at_near = core * 2 + bit, (1 - core) * 2 + bit_near
    places = (at, at_near, at ^ 1, at_near ^ 1)
    always = d + t < replicas + tensor

    def together(steps, *args):
        def skipped(*args):
            shapes = jax.eval_shape(steps, *args)
            return jax.tree.map(lambda v: jnp.zeros(v.shape, v.dtype), shapes)

        return lax.cond(always, steps, skipped, *args)

    xa0 = cross(layer_input, 0)

    def project_rows(x, r):
        x_near = swap(x)
        y = project(tie(x, r), r)
        y_near = swap(y)
        return x_near, y, y_near, jnp.concatenate([y, y_near], axis=0)

    x_near, y, y_near, pair = together(project_rows, layer_input, right_factor)

    def exchange(pair, r, errors):
        y_far = cross(pair, 1)
        e = feedback(tie(r, pair), errors)
        return tie(y_far, e), e

    y_far, e = together(exchange, pair, right_factor, errors)
    xb0 = cross(tie(x_near, y_far), 0)

    def left_factors(y, y_near, y_far, e):
        left = left_local(place, (y, y_near, swap(y_far), y_far), kv_cotangent, e)
        grads = []
        for k in range(bits):
            arrived = hop(left, k)
            if k < 2:
                grads.append(grad_half(k, place, kv_cotangent, tie(kv_weight, left)))
                arrived = tie(arrived, grads[k][0])
            if k == 1:
                got0 = swap(tie(grads[0][1], left))
                arrived = tie(arrived, got0)
            elif k == 2:
                got1 = swap(tie(grads[1][1], left))
                own0, first = pair_sum(grads[0][0], tie(got0, left), (1,))
                arrived = tie(arrived, first, got1)
            left = left + arrived
        return left, grads[1][0], got1, own0, first

    left, keep1, got1, own0, first = together(left_factors, y, y_near, y_far, e)
    left, xa0 = lax.optimization_barrier((left, xa0))

    def spread_out(left, keep1, got1, xa0):
        own, send, far = spread(place, left, kv_cotangent)
        near = swap(jnp.concatenate([send, far], axis=0))
        chip = far + near[n:]
        got = cross(chip, 1)
        xa1 = swap(tie(xa0, chip))
        own1, *pieces = pair_sum(tie(keep1, chip), got1, SECOND_PIECES)
        got = tie(got, xa1, own1, *pieces)
        return own, near[:n], chip, swap(got), got, own1, pieces, xa1

    own, near, chip, *gots, own1, (second, third), xa1 = together(spread_out, left, keep1, got1, xa0)
    first = cross(tie(first, chip))
    second = cross(tie(second, chip))
    chip, xb0 = lax.optimization_barrier((chip, xb0))

    def moments_of(j, xs, after, *so_far):
        return moment_quarter(j, place, xs, tie(kv_cotangent, after), errors, so_far)

    def right_sums(own, near, chip, got0, got, left, x_near, xa0, xa1, xb0):
        xb1 = swap(xb0)
        z, b = solve(place, own, near, chip, got0, got, left)
        half_near, half = right_halves(core, bit, bit_near, z, b, layer_input, errors)
        half_near = swap(tie(half_near, xb1))
        quarter = half.shape[1] // 2
        give = (half[:, :quarter] + half_near[:, :quarter]).astype(BF16)
        xs = (layer_input, x_near, xa0, xa1, xb0, xb1)
        moments = moments_of(0, xs, give)
        own = half[:, quarter:] + half_near[:, quarter:] + tie(hop(give, 0), moments).astype(F32)
        for k in range(1, bits):
            rounded = lax.optimization_barrier(own.astype(BF16))
            moments = moments_of(k, xs, rounded, moments)
            own = rounded.astype(F32) + tie(hop(rounded, k), moments).astype(F32)
        return own.astype(BF16), b, moments, xb1

    args = (own, near, chip, *gots, left, x_near, xa0, xa1, xb0)
    own, b, moments, xb1 = together(right_sums, *args)
    xs = (layer_input, x_near, xa0, xa1, xb0, xb1)
    own, first, second = lax.optimization_barrier((own, first, second))

    def last_quarters(own, third, b, moments, xs, own0, first):
        arrived = cross(own)
        moments = moments_of(3, xs, own, moments)
        own = own.astype(F32) + tie(arrived, moments).astype(F32)
        own = lax.optimization_barrier((own * (1.0 / replicas)).astype(BF16))
        third = cross(tie(third, own))
        other = hop(own, 0)
        near = swap(own)
        after, right = error_quarters(places[:2], moments, (own, near), b)
        other = tie(other, right)
        other_near = swap(other)
        grad = finish_grad(0, own0, (tie(first, other),))
        other_near = tie(other_near, grad)
        return *error_quarters(places[2:], after, (other, other_near), b, (right,)), grad, third

    after, right, grad, third = together(last_quarters, own, third, b, moments, xs, own0, first)
    grad = finish_grad(1, vmem(own1), (vmem(second), third), (grad,))
    return (after[None], right.reshape(right_factor.shape), grad)


def solution(mesh):
    sizes = mesh.shape
    fits = sizes["tensor"] == 4 and sizes["dp"] == 8
    return jax.shard_map(
        per_device if fits else any_mesh,
        mesh=mesh,
        in_specs=(
            P(("dp", "tensor"), None),
            P(None, None, "tensor"),
            P(None, "dp", "tensor"),
            P("dp", None, None, "tensor"),
            P(),
        ),
        out_specs=(P("dp", None, None, "tensor"), P(), P(("dp", "tensor"), None)),
        check_vma=False,
    )
```

```python
from functools import partial

import jax
import jax.numpy as jnp
from jax import lax
from jax.experimental import pallas as pl
from jax.experimental.pallas import tpu as pltpu
from jax.sharding import PartitionSpec as P

TOKENS = 1024
SCALE = TOKENS ** (-0.5)
F32, BF16 = jnp.float32, jnp.bfloat16
WEIGHT = 4096
MOMENT_STEPS = 2
SECOND_PIECES = (6, 10)
VMEM_LIMIT = 12 * 1024 * 1024
NN = (((1,), (0,)), ((), ()))
NT = (((1,), (1,)), ((), ()))
TN = (((0,), (0,)), ((), ()))
HIGHEST = lax.Precision.HIGHEST


def mm(a, b, dims, precision=None):
    return lax.dot_general(a, b, dims, precision=precision, preferred_element_type=F32)


def split(value, terms):
    parts, rest = [], value
    for _ in range(terms):
        part = rest.astype(BF16)
        parts.append(part)
        rest = rest - part.astype(F32)
    return jnp.concatenate(parts, axis=0)


def split_mm(a, b, dims, terms):
    rows = a.shape[0]
    product = mm(split(a, terms), b, dims)
    total = product[:rows]
    for k in range(1, terms):
        total = total + product[k * rows : (k + 1) * rows]
    return total


def params(*semantics):
    return pltpu.CompilerParams(
        vmem_limit_bytes=VMEM_LIMIT,
        dimension_semantics=semantics if semantics else None,
    )


SMEM = pl.BlockSpec(memory_space=pltpu.SMEM)
VMEM = pl.BlockSpec(memory_space=pltpu.VMEM)


def vmem(value):
    return pltpu.with_memory_space_constraint(value, pltpu.VMEM)


def hbm(value):
    return pltpu.with_memory_space_constraint(value, pltpu.HBM)


def cost(flops, nbytes):
    return pl.CostEstimate(flops=int(flops) // WEIGHT, bytes_accessed=int(nbytes) // WEIGHT, transcendentals=0)


def project_kernel(x_ref, r_ref, y_ref):
    modes, rank, chunk = r_ref.shape
    term = split_mm(r_ref[...].reshape(modes * rank, chunk), x_ref[...], NT, 3)

    @pl.when(pl.program_id(0) == 0)
    def _():
        y_ref[...] = term

    @pl.when(pl.program_id(0) > 0)
    def _():
        y_ref[...] += term


def project(x, r, chunk=2048):
    rows, depth = x.shape
    modes, rank, _ = r.shape
    return pl.pallas_call(
        project_kernel,
        grid=(depth // chunk,),
        in_specs=[
            pl.BlockSpec((rows, chunk), lambda i: (0, i)),
            pl.BlockSpec((modes, rank, chunk), lambda i: (0, 0, i)),
        ],
        out_specs=pl.BlockSpec((modes * rank, rows), lambda i: (0, 0)),
        out_shape=jax.ShapeDtypeStruct((modes * rank, rows), F32),
        compiler_params=params("arbitrary"),
        cost_estimate=cost(6 * rows * depth * modes * rank, x.nbytes + r.nbytes),
        name="project",
    )(hbm(x), hbm(r))


def feedback_kernel(r_ref, e_ref, out_ref):
    term = split_mm(r_ref[0], e_ref[0], NN, 3)

    @pl.when(pl.program_id(1) == 0)
    def _():
        out_ref[...] = term

    @pl.when(pl.program_id(1) > 0)
    def _():
        out_ref[...] += term


def feedback(r, e, chunk=4096):
    modes, rank, depth = r.shape
    cols = e.shape[-1]
    return pl.pallas_call(
        feedback_kernel,
        grid=(modes, depth // chunk),
        in_specs=[
            pl.BlockSpec((1, rank, chunk), lambda m, i: (m, 0, i)),
            pl.BlockSpec((1, chunk, cols), lambda m, i: (m, i, 0)),
        ],
        out_specs=pl.BlockSpec((rank, cols), lambda m, i: (m, 0)),
        out_shape=jax.ShapeDtypeStruct((modes * rank, cols), F32),
        compiler_params=params("arbitrary", "arbitrary"),
        cost_estimate=cost(6 * modes * rank * depth * cols, r.nbytes + e.nbytes),
        name="feedback",
    )(hbm(r), hbm(e))


def rows_of(t_ref, j, rows):
    return pl.ds(pl.multiple_of((t_ref[0] ^ j) * rows, rows), rows)


def by_core(t_ref, on_core0, on_core1):
    return jnp.where(t_ref[0] % 2 == 0, on_core0, on_core1)


def left_kernel(t_ref, own, near, far0, far1, g_ref, e_ref, out_ref):
    modes = g_ref.shape[0]
    rank, rows = own.shape[0] // modes, own.shape[1]
    n = modes * rank
    far = by_core(t_ref, far0[...], far1[...])
    same = by_core(t_ref, far[n:], far[:n])
    other = by_core(t_ref, far[:n], far[n:])
    for m in range(modes):
        at = slice(m * rank, (m + 1) * rank)
        total = 0.0
        for j, y in enumerate((own[...], near[...], same, other)):
            total = total + split_mm(y[at], g_ref[m, rows_of(t_ref, j, rows), :], NN, 3)
        out_ref[at, :] = total * SCALE + e_ref[at, :]


def left_local(t, ys, g, e):
    return pl.pallas_call(
        left_kernel,
        in_specs=[SMEM] + [VMEM] * 6,
        out_specs=VMEM,
        out_shape=jax.ShapeDtypeStruct(e.shape, F32),
        compiler_params=params(),
        cost_estimate=cost(6 * e.size * g.shape[1], g.nbytes),
        name="left",
    )(t, *ys, g, e)


def spread_kernel(t_ref, left_ref, g_ref, own_ref, near_ref, far_ref):
    modes = g_ref.shape[0]
    rank = left_ref.shape[0] // modes
    rows = own_ref.shape[1]
    n = modes * rank
    low = 2 + t_ref[0] % 2
    for j, (ref, top) in ((0, (own_ref, 0)), (1, (near_ref, 0)), (low, (far_ref, 0)), (low ^ 1, (far_ref, n))):
        for m in range(modes):
            ref[top + m * rank : top + (m + 1) * rank, :] = split_mm(
                left_ref[m * rank : (m + 1) * rank, :], g_ref[m, rows_of(t_ref, j, rows), :], NT, 3
            )
    zero = jnp.zeros((rank, left_ref.shape[1]), F32)
    a, b = left_ref[0:rank, :], left_ref[rank : 2 * rank, :]
    gram = mm(a, jnp.concatenate([a, zero, zero, zero], axis=0), NT, HIGHEST)
    gram = gram + mm(b, jnp.concatenate([zero, zero, b, zero], axis=0), NT, HIGHEST)
    far_ref[2 * n :, 0:128] = gram[: rank // 2]
    far_ref[2 * n :, 128:] = gram[rank // 2 :]


def spread(t, left, g):
    rows = g.shape[1] // 4
    n = left.shape[0]
    small = jax.ShapeDtypeStruct((n, rows), F32)
    return pl.pallas_call(
        spread_kernel,
        in_specs=[SMEM, VMEM, VMEM],
        out_specs=[VMEM, VMEM, VMEM],
        out_shape=[small, small, jax.ShapeDtypeStruct((2 * n + n // 4, rows), F32)],
        compiler_params=params(),
        cost_estimate=cost(6 * left.size * g.shape[1], g.nbytes),
        name="spread",
    )(t, left, g)


def solve_kernel(t_ref, own_ref, near_ref, chip_ref, got0, got1, left_ref, z_ref, b_ref):
    modes = 2
    rank = left_ref.shape[0] // modes
    n = modes * rank
    got = by_core(t_ref, got0[...], got1[...])
    gram = chip_ref[2 * n :, :] + got[2 * n :, :]
    gram = jnp.concatenate([gram[:, 0:128], gram[:, 128:]], axis=0)
    row = lax.broadcasted_iota(jnp.int32, (rank, 128), 0)
    lane = lax.broadcasted_iota(jnp.int32, (rank, 128), 1)
    ones = jnp.where((lane == row + rank) | (lane == row + 3 * rank), 1.0, 0.0)
    a = jnp.where((lane // rank) % 2 == 0, gram, ones)
    low = lane < 2 * rank
    scale = jnp.zeros((rank, 128), F32)
    for k in range(rank):
        pivot_row = a[k : k + 1, :]
        column = jnp.where(low, a[:, k : k + 1], a[:, 2 * rank + k : 2 * rank + k + 1])
        pivot = column[k : k + 1, :]
        inverse = 1.0 / pivot
        scale = jnp.where(row == k, lax.rsqrt(pivot), scale)
        a = jnp.where(row > k, a - column * (inverse * pivot_row), a)
    a = a * scale
    zero = jnp.zeros((rank, left_ref.shape[1]), F32)
    z = (own_ref[...] + near_ref[0:n, :] + by_core(t_ref, got[0:n], got[n : 2 * n])) * SCALE
    for m in range(modes):
        part = jnp.where(lane // rank == 2 * m + 1, a, 0.0)
        at = slice(m * rank, (m + 1) * rank)
        for value, ref in ((z[at], z_ref), (left_ref[at, :], b_ref)):
            stacked = [zero] * 4
            stacked[2 * m + 1] = value
            ref[at, :] = mm(part, jnp.concatenate(stacked, axis=0), NN, HIGHEST)


def solve(t, own, near, chip, got0, got1, left):
    shape = jax.ShapeDtypeStruct(left.shape, F32)
    return pl.pallas_call(
        solve_kernel,
        in_specs=[SMEM] + [VMEM] * 6,
        out_specs=[VMEM, VMEM],
        out_shape=[shape, shape],
        compiler_params=params(),
        cost_estimate=cost(10**7, 10**7),
        name="solve",
    )(t, own, near, chip, got0, got1, left)


def right_kernel(h_ref, z_ref, b_ref, x_ref, e_ref, near_ref, own_ref):
    modes, width, _ = e_ref.shape
    rank = z_ref.shape[0] // modes
    product = split_mm(z_ref[...], x_ref[...], NN, 2)
    parts = []
    for m in range(modes):
        at = slice(m * rank, (m + 1) * rank)
        parts.append(product[at] + split_mm(b_ref[at, :], e_ref[m], NT, 2))
    whole = jnp.concatenate(parts, axis=0)
    low, high = whole[:, : width // 2], whole[:, width // 2 :]
    i = pl.program_id(0)
    keep_high = h_ref[2 + i] == 1
    ordered = jnp.concatenate([jnp.where(keep_high, low, high), jnp.where(keep_high, high, low)], axis=1)

    @pl.when(i == 0)
    def _():
        near_ref[...] = ordered

    @pl.when(i == 1)
    def _():
        own_ref[...] = ordered


def right_halves(core, bit, bit_near, z, b, x, e):
    rows, depth = x.shape
    modes, _, cols = e.shape
    width = depth // 2
    shape = jax.ShapeDtypeStruct((z.shape[0], width), F32)
    whole = pl.BlockSpec(shape.shape, lambda i, h: (0, 0))
    return pl.pallas_call(
        right_kernel,
        grid_spec=pltpu.PrefetchScalarGridSpec(
            num_scalar_prefetch=1,
            grid=(2,),
            in_specs=[
                pl.BlockSpec(z.shape, lambda i, h: (0, 0)),
                pl.BlockSpec(b.shape, lambda i, h: (0, 0)),
                pl.BlockSpec((rows, width), lambda i, h: (0, h[i])),
                pl.BlockSpec((modes, width, cols), lambda i, h: (0, h[i], 0)),
            ],
            out_specs=[whole, whole],
        ),
        out_shape=[shape, shape],
        compiler_params=params("arbitrary"),
        cost_estimate=cost(8 * depth * rows * 128, x.nbytes + e.nbytes),
        name="right",
    )(jnp.stack([1 - core, core, bit_near, bit]), z, b, hbm(x), hbm(e))


def moment_kernel(t_ref, x0, x1, a0, a1, b0, b1, g_ref, e_ref, *refs):
    out_ref = refs[-1]
    modes = g_ref.shape[0]
    rows = x0.shape[0]
    low = 2 + t_ref[0] % 2
    terms = ((0, x0[...]), (1, x1[...]), (low, by_core(t_ref, a0[...], a1[...])), (low ^ 1, by_core(t_ref, b0[...], b1[...])))
    for m in range(modes):
        total = 0.0
        for j, x in terms:
            total = total + mm(x, g_ref[m, rows_of(t_ref, j, rows), :], TN)
        out_ref[m] = total * SCALE + e_ref[m].astype(F32)


def moment_quarter(quarter, t, xs, g, e, so_far=()):
    rows, depth = xs[0].shape
    modes, tokens, cols = g.shape
    steps = MOMENT_STEPS
    chunk = depth // 4 // steps
    first = steps * quarter
    both = pl.BlockSpec((rows, chunk), lambda i, t: (0, first + i))
    on0 = pl.BlockSpec((rows, chunk), lambda i, t: (0, (first + i) * (1 - t[0] % 2)))
    on1 = pl.BlockSpec((rows, chunk), lambda i, t: (0, (first + i) * (t[0] % 2)))
    return pl.pallas_call(
        moment_kernel,
        grid_spec=pltpu.PrefetchScalarGridSpec(
            num_scalar_prefetch=1,
            grid=(steps,),
            in_specs=[
                both,
                both,
                on0,
                on1,
                on0,
                on1,
                pl.BlockSpec(g.shape, lambda i, t: (0, 0, 0)),
                pl.BlockSpec((modes, chunk, cols), lambda i, t: (0, first + i, 0)),
            ]
            + [pl.BlockSpec(memory_space=pl.ANY)] * len(so_far),
            out_specs=pl.BlockSpec((modes, chunk, cols), lambda i, t: (0, first + i, 0)),
        ),
        out_shape=pltpu.HBM((modes, depth, cols), F32),
        input_output_aliases={9: 0} if so_far else {},
        compiler_params=params("arbitrary"),
        cost_estimate=cost(2 * depth * modes * cols * tokens // 4, 8 * 2**20),
        name="moment",
    )(t, *xs, g, hbm(e), *so_far)


def error_kernel(q_ref, m_ref, r0, r1, b_ref, *refs):
    out_ref, right_ref = refs[-2:]
    modes = out_ref.shape[0]
    rank = b_ref.shape[0] // modes
    right = jnp.where(pl.program_id(0) == 0, r0[...], r1[...])
    right_ref[...] = right.astype(F32)
    for m in range(modes):
        at = slice(m * rank, (m + 1) * rank)
        stacked = jnp.concatenate([right[at], right[at]], axis=0)
        out_ref[m] = m_ref[m] - mm(stacked, split(b_ref[at, :], 2), TN)


def error_quarters(places, moments, rights, b, so_far=(), pieces=1):
    modes, depth, cols = moments.shape
    ranks, width = rights[0].shape
    width //= pieces
    spec = pl.BlockSpec((modes, width, cols), lambda i, j, q: (0, q[i] * pieces + j, 0))
    half = pl.BlockSpec((ranks, width), lambda i, j, q: (0, j))
    return pl.pallas_call(
        error_kernel,
        grid_spec=pltpu.PrefetchScalarGridSpec(
            num_scalar_prefetch=1,
            grid=(2, pieces),
            in_specs=[spec, half, half, pl.BlockSpec(b.shape, lambda i, j, q: (0, 0))]
            + [pl.BlockSpec(memory_space=pl.ANY)] * len(so_far),
            out_specs=[spec, pl.BlockSpec((ranks, width), lambda i, j, q: (0, q[i] * pieces + j))],
        ),
        out_shape=[
            pltpu.HBM(moments.shape, F32),
            pltpu.HBM((ranks, depth), F32),
        ],
        input_output_aliases={1: 0, 5: 1} if so_far else {1: 0},
        compiler_params=params("arbitrary", "arbitrary"),
        cost_estimate=cost(10**6, 8 * 2**20),
        name="error",
    )(jnp.stack(places), moments, *rights, b, *so_far)


def grad_kernel(t_ref, g_ref, w_ref, keep_ref, send_ref):
    rows = keep_ref.shape[0] // 2
    w = jnp.concatenate([w_ref[0], w_ref[1]], axis=1)
    for j, (ref, top) in enumerate(((keep_ref, 0), (send_ref, 0), (keep_ref, rows), (send_ref, rows))):
        at = rows_of(t_ref, j, rows)
        g = jnp.concatenate([g_ref[0, at, :], g_ref[1, at, :]], axis=1)
        ref[top : top + rows, :] = mm(g, w, NT).astype(BF16)


def grad_half(half, t, g, w, chunk=1024):
    modes, depth, cols = w.shape
    rows = g.shape[1] // 2
    steps = depth // 2 // chunk
    first = half * steps
    shape = jax.ShapeDtypeStruct((rows, depth // 2), BF16)
    return pl.pallas_call(
        grad_kernel,
        grid=(steps,),
        in_specs=[
            SMEM,
            pl.BlockSpec(g.shape, lambda i: (0, 0, 0)),
            pl.BlockSpec((modes, chunk, cols), lambda i: (0, first + i, 0)),
        ],
        out_specs=[pl.BlockSpec((rows, chunk), lambda i: (0, i))] * 2,
        out_shape=[shape, shape],
        compiler_params=params("arbitrary"),
        cost_estimate=cost(4 * rows * depth * modes * cols, w.nbytes),
        name="grad",
    )(t, g, hbm(w))


def pair_kernel(a0, b0, a1, b1, own_ref, *outs):
    own_ref[...] = (a0[...].astype(F32) + b0[...].astype(F32)).astype(BF16)
    total = (a1[...].astype(F32) + b1[...].astype(F32)).astype(BF16)
    first = 0
    for out in outs:
        out[...] = total[:, first : first + out.shape[1]]
        first += out.shape[1]


def pair_sum(a, b, sizes, steps=2):
    rows, width = a.shape
    rows //= 2
    widths = [width] + [width * size // sum(sizes) for size in sizes]
    own = pl.BlockSpec((rows // steps, width), lambda i: (i, 0))
    far = pl.BlockSpec((rows // steps, width), lambda i: (steps + i, 0))
    return pl.pallas_call(
        pair_kernel,
        grid=(steps,),
        in_specs=[own, own, far, far],
        out_specs=[pl.BlockSpec((rows // steps, w), lambda i: (i, 0)) for w in widths],
        out_shape=[jax.ShapeDtypeStruct((rows, w), BF16) for w in widths],
        compiler_params=params("arbitrary"),
        cost_estimate=cost(2 * rows * width, 12 * rows * width),
        name="pair_sum",
    )(a, b, a, b)


def finish_kernel(count, own_ref, *refs):
    out_ref = refs[-1]
    first = 0
    for far_ref in refs[:count]:
        at = slice(first, first + far_ref.shape[1])
        out_ref[:, at] = (own_ref[:, at].astype(F32) + far_ref[...].astype(F32)).astype(BF16)
        first = at.stop


def finish_grad(half, own, fars, so_far=(), steps=2):
    rows, width = own.shape
    return pl.pallas_call(
        partial(finish_kernel, len(fars)),
        grid=(steps,),
        in_specs=[pl.BlockSpec((rows // steps, width), lambda i: (i, 0))]
        + [pl.BlockSpec((rows // steps, far.shape[1]), lambda i: (i, 0)) for far in fars]
        + [pl.BlockSpec(memory_space=pl.ANY)] * len(so_far),
        out_specs=pl.BlockSpec((rows // steps, width), lambda i: (i, half)),
        out_shape=pltpu.HBM((rows, 2 * width), BF16),
        input_output_aliases={1 + len(fars): 0} if so_far else {},
        compiler_params=params("arbitrary"),
        cost_estimate=cost(3 * rows * width, 8 * rows * width),
        name="finish_grad",
    )(own, *fars, *so_far)


def compress(moments, right_prev):
    highest = lax.Precision.HIGHEST
    replicas = lax.axis_size("dp")
    projected = jnp.einsum("mdc,mrd->mrc", moments, right_prev, precision=highest)
    left_sum = lax.psum(projected, "dp")
    gram_matrix = lax.psum(
        jnp.einsum("mrc,msc->mrs", left_sum, left_sum, precision=highest), "tensor"
    )
    factor = jnp.linalg.cholesky(gram_matrix)
    ortho_basis = jax.vmap(partial(jax.scipy.linalg.solve_triangular, lower=True))(factor, left_sum)
    right_local = jnp.einsum("mdc,mrc->mrd", moments, ortho_basis, precision=highest)
    right_total = lax.psum(right_local, "tensor")
    right_total = lax.psum(right_total, "dp")
    right_mean = right_total / replicas
    approximation = jnp.einsum("mrd,mrc->mdc", right_mean, ortho_basis, precision=highest)
    return (moments - approximation, right_mean)


def any_mesh(layer_input, kv_weight, kv_cotangent, error_before, right_factor):
    portion = kv_cotangent
    weight_grad = jnp.einsum(
        "td,mtc->mdc",
        lax.all_gather(layer_input, "tensor", axis=0, tiled=True),
        portion,
        preferred_element_type=jnp.float32,
    )
    moments = weight_grad * TOKENS ** (-0.5) + error_before[0].astype(jnp.float32)
    portion = kv_cotangent
    input_sum = lax.psum_scatter(
        jnp.einsum("mtc,mdc->td", portion, kv_weight, preferred_element_type=jnp.float32).astype(
            jnp.bfloat16
        ),
        "tensor",
        scatter_dimension=0,
        tiled=True,
    )
    leading = compress(moments[0:1], right_factor[0:1])
    second = compress(moments[1:2], right_factor[1:2])
    errors = jnp.concatenate([leading[0], second[0]], axis=0)
    right_next = jnp.concatenate([leading[1], second[1]], axis=0)
    return (errors[None], right_next, input_sum)


def tie(value, *others):
    return lax.optimization_barrier((value, *others))[0]


def per_device(layer_input, kv_weight, kv_cotangent, error_before, right_factor):
    tensor, replicas = lax.axis_size("tensor"), lax.axis_size("dp")
    t = lax.axis_index("tensor").astype(jnp.int32)
    d = lax.axis_index("dp").astype(jnp.int32)
    core = t & 1
    place = t.reshape(1)
    errors = error_before[0]
    depth = layer_input.shape[1]
    n = 2 * right_factor.shape[1]
    bits = replicas.bit_length() - 1

    def swap(value):
        return lax.ppermute(value, "tensor", [(i, i ^ 1) for i in range(tensor)])

    def cross(value, carrier=None):
        cores = range(tensor) if carrier is None else range(carrier, tensor, 2)
        return lax.ppermute(value, "tensor", [(i, i ^ 2) for i in cores])

    def hop(value, step):
        pairs = []
        for i in range(replicas):
            for k in range(tensor):
                bit = (step + 1 - k % 2) % bits
                pairs.append((i * tensor + k, (i ^ (1 << bit)) * tensor + k))
        return lax.ppermute(value, ("dp", "tensor"), pairs)

    bit0, bit1 = (d >> (1 % bits)) & 1, d & 1
    bit, bit_near = jnp.where(core == 1, bit1, bit0), jnp.where(core == 1, bit0, bit1)
    at, at_near = core * 2 + bit, (1 - core) * 2 + bit_near
    places = (at, at_near, at ^ 1, at_near ^ 1)
    always = d + t < replicas + tensor

    def together(steps, *args):
        def skipped(*args):
            shapes = jax.eval_shape(steps, *args)
            return jax.tree.map(lambda v: jnp.zeros(v.shape, v.dtype), shapes)

        return lax.cond(always, steps, skipped, *args)

    xa0 = cross(layer_input, 0)

    def project_rows(x, r):
        x_near = swap(x)
        y = project(tie(x, r), r)
        y_near = swap(y)
        return x_near, y, y_near, jnp.concatenate([y, y_near], axis=0)

    x_near, y, y_near, pair = together(project_rows, layer_input, right_factor)

    def exchange(pair, r, errors):
        y_far = cross(pair, 1)
        e = feedback(tie(r, pair), errors)
        return tie(y_far, e), e

    y_far, e = together(exchange, pair, right_factor, errors)
    xb0 = cross(tie(x_near, y_far), 0)

    def left_factors(y, y_near, y_far, e):
        left = left_local(place, (y, y_near, swap(y_far), y_far), kv_cotangent, e)
        grads = []
        for k in range(bits):
            arrived = hop(left, k)
            if k < 2:
                grads.append(grad_half(k, place, kv_cotangent, tie(kv_weight, left)))
                arrived = tie(arrived, grads[k][0])
            if k == 1:
                got0 = swap(tie(grads[0][1], left))
                arrived = tie(arrived, got0)
            elif k == 2:
                got1 = swap(tie(grads[1][1], left))
                own0, first = pair_sum(grads[0][0], tie(got0, left), (1,))
                arrived = tie(arrived, first, got1)
            left = left + arrived
        return left, grads[1][0], got1, own0, first

    left, keep1, got1, own0, first = together(left_factors, y, y_near, y_far, e)
    left, xa0 = lax.optimization_barrier((left, xa0))

    def spread_out(left, keep1, got1, xa0):
        own, send, far = spread(place, left, kv_cotangent)
        near = swap(jnp.concatenate([send, far], axis=0))
        chip = far + near[n:]
        got = cross(chip, 1)
        xa1 = swap(tie(xa0, chip))
        own1, *pieces = pair_sum(tie(keep1, chip), got1, SECOND_PIECES)
        got = tie(got, xa1, own1, *pieces)
        return own, near[:n], chip, swap(got), got, own1, pieces, xa1

    own, near, chip, *gots, own1, (second, third), xa1 = together(spread_out, left, keep1, got1, xa0)
    first = cross(tie(first, chip))
    second = cross(tie(second, chip))
    chip, xb0 = lax.optimization_barrier((chip, xb0))

    def moments_of(j, xs, after, *so_far):
        return moment_quarter(j, place, xs, tie(kv_cotangent, after), errors, so_far)

    def right_sums(own, near, chip, got0, got, left, x_near, xa0, xa1, xb0):
        xb1 = swap(xb0)
        z, b = solve(place, own, near, chip, got0, got, left)
        half_near, half = right_halves(core, bit, bit_near, z, b, layer_input, errors)
        half_near = swap(tie(half_near, xb1))
        quarter = half.shape[1] // 2
        give = (half[:, :quarter] + half_near[:, :quarter]).astype(BF16)
        xs = (layer_input, x_near, xa0, xa1, xb0, xb1)
        moments = moments_of(0, xs, give)
        own = half[:, quarter:] + half_near[:, quarter:] + tie(hop(give, 0), moments).astype(F32)
        for k in range(1, bits):
            rounded = lax.optimization_barrier(own.astype(BF16))
            moments = moments_of(k, xs, rounded, moments)
            own = rounded.astype(F32) + tie(hop(rounded, k), moments).astype(F32)
        return own.astype(BF16), b, moments, xb1

    args = (own, near, chip, *gots, left, x_near, xa0, xa1, xb0)
    own, b, moments, xb1 = together(right_sums, *args)
    xs = (layer_input, x_near, xa0, xa1, xb0, xb1)
    own, first, second = lax.optimization_barrier((own, first, second))

    def last_quarters(own, third, b, moments, xs, own0, first):
        arrived = cross(own)
        moments = moments_of(3, xs, own, moments)
        own = own.astype(F32) + tie(arrived, moments).astype(F32)
        own = lax.optimization_barrier((own * (1.0 / replicas)).astype(BF16))
        third = cross(tie(third, own))
        other = hop(own, 0)
        near = swap(own)
        after, right = error_quarters(places[:2], moments, (own, near), b)
        other = tie(other, right)
        other_near = swap(other)
        grad = finish_grad(0, own0, (tie(first, other),))
        other_near = tie(other_near, grad)
        return *error_quarters(places[2:], after, (other, other_near), b, (right,)), grad, third

    after, right, grad, third = together(last_quarters, own, third, b, moments, xs, own0, first)
    grad = finish_grad(1, vmem(own1), (vmem(second), third), (grad,))
    return (after[None], right.reshape(right_factor.shape), grad)


def solution(mesh):
    sizes = mesh.shape
    fits = sizes["tensor"] == 4 and sizes["dp"] == 8
    return jax.shard_map(
        per_device if fits else any_mesh,
        mesh=mesh,
        in_specs=(
            P(("dp", "tensor"), None),
            P(None, None, "tensor"),
            P(None, "dp", "tensor"),
            P("dp", None, None, "tensor"),
            P(),
        ),
        out_specs=(P("dp", None, None, "tensor"), P(), P(("dp", "tensor"), None)),
        check_vma=False,
    )
```
